32 devices in a mesh: member: 2 (over y), tile: 4 (over z), nest: 2 (over x), lev: 2 (over core).
Axes of the slice: x: 2, y: 2, z: 4, core: 2. Of those that a mesh axis runs over, the one named last changes fastest.
Arguments:
- parent_field: float32 [10, 2, 256, 512], P('member', None, 'tile', ('nest', 'lev')), parts along dimension 0, may hold values from -6 to 6
- nest_fields: float32 [12, 5, 2, 384, 384], P(('member', 'nest'), None, None, 'tile', 'lev'), parts along dimension 0, may hold values from -6 to 6
- lateral_rate: float32 [5], replicated, may hold values from 0.02 to 0.12
- vertical_rate: float32 [5], replicated, may hold values from 0.02 to 0.12
- centres: int32 [6, 6, 2], P('member'), parts along dimension 0, may hold values from 64 to 448, as said below
- slot_storm: int32 [12], P('member'), parts along dimension 0, may hold values from 0 to 5, each once
Outputs:
- parent_final: float32 [10, 2, 256, 512], P('member', None, 'tile', ('nest', 'lev')), parts along dimension 0
- nest_final: float32 [12, 5, 2, 384, 384], P(('member', 'nest'), None, None, 'tile', 'lev'), parts along dimension 0
The draws below stay inside these ranges and needn't reach their ends.
There are 2 independent parts, one for each index of `member`. The reference program is written for one: setup_inputs(seed, part) draws one part's arguments, and reference() takes and returns one part's arrays. A program takes and returns all parts, laid end to end along the dimension named above; an argument that names none is the same for every part. Nothing has to cross between parts.
Inputs may be any that keep to these rules, and one draw needn't show every extreme that they name: `centres`: from one step to the next the row of a centre changes by 1 to 2 cells in either direction and the column by at most 2 cells; rows stay within 64 to 192 and columns within 64 to 448. `slot_storm`: every storm occupies exactly one nest position.
All inputs are finite; a program needn't handle non-finite values.
Results may differ from the reference program's by a relative error of at most 0.0003.
Values sent between devices are 32-bit elements; how exact they have to be, the bound alone decides.
A program may use at most 128 MiB of HBM per device.

```python
import math
import jax
import jax.numpy as jnp
from jax import lax

F = 5
LEV = 2
NXP = 256
NYP = 512
FP = 128
NXN = 384
NESTS = 6
BWP = 2
MOVE = 2
STEPS = 2


def draw_centres(key, part):
    half_span = FP // 2
    travel = MOVE * STEPS
    key_rows = jax.random.fold_in(key, 11)
    key_cols = jax.random.fold_in(key, 12)
    key_size = jax.random.fold_in(key, 13)
    key_sign = jax.random.fold_in(key, 14)
    key_drift = jax.random.fold_in(key, 15)
    first_rows = jax.random.randint(key_rows, (NESTS,), half_span + travel, NXP - half_span - travel + 1, dtype=jnp.int32)
    first_cols = jax.random.randint(key_cols, (NESTS,), half_span + travel, NYP - half_span - travel + 1, dtype=jnp.int32)
    row_size = jax.random.randint(key_size, (STEPS, NESTS), 1, MOVE + 1, dtype=jnp.int32)
    row_sign = 2 * jax.random.randint(key_sign, (STEPS, NESTS), 0, 2, dtype=jnp.int32) - 1
    row_moves = row_size * row_sign
    col_moves = jax.random.randint(key_drift, (STEPS, NESTS), -MOVE, MOVE + 1, dtype=jnp.int32)
    first_rows = first_rows.at[0].set(half_span + travel)
    row_moves = row_moves.at[:, 0].set(-MOVE)
    if NXP >= NYP:
        first_rows = first_rows.at[1].set(NXP - half_span - travel)
        row_moves = row_moves.at[:, 1].set(MOVE)
    else:
        first_cols = first_cols.at[1].set(NYP - half_span - travel)
        col_moves = col_moves.at[:, 1].set(MOVE)
    row_track = jnp.concatenate([first_rows[None, :], first_rows[None, :] + jnp.cumsum(row_moves, axis=0)], axis=0)
    col_track = jnp.concatenate([first_cols[None, :], first_cols[None, :] + jnp.cumsum(col_moves, axis=0)], axis=0)
    return jnp.stack([row_track, col_track], axis=-1).astype(jnp.int32)


def block_scale(stream_key, dims, shards, smallest, high):
    loudness = 1.0
    for position, parts in shards:
        steps = jax.random.uniform(jax.random.fold_in(jax.random.fold_in(stream_key, 6), position), (parts,), jnp.float32, smallest / len(shards), high / len(shards))
        loudness = loudness * jnp.repeat(jnp.exp(steps), dims[position] // parts).reshape((-1,) + (1,) * (len(dims) - 1 - position))
    return loudness


def normal_values(stream_key, dims, spread, bound, shards=(), held_as=jnp.bfloat16):
    values = jax.random.normal(stream_key, dims, jnp.float32) * spread
    if len(shards) > 0:
        values = block_scale(stream_key, dims, shards, -0.22, 0.18) * values
    return jnp.clip(values, min=-bound, max=bound).astype(held_as)


def setup_inputs(seed: int = 0, part: int = 0) -> dict:
    seeds = jax.random.split(jax.random.key(seed), 7)
    own_keys = jax.random.split(jax.random.fold_in(seeds[6], part), 7)
    parent_field = normal_values(own_keys[0], (F, LEV, NXP, NYP), 1.0, 6.0, ((2, 4), (3, 4)), jnp.float32)
    nest_fields = normal_values(own_keys[1], (NESTS, F, LEV, NXN, NXN), 1.0, 6.0, ((0, 2), (3, 4), (4, 2)), jnp.float32)
    lateral_rate = jnp.clip(jnp.exp(jax.random.uniform(seeds[2], (F,), jnp.float32, math.log(0.02), math.log(0.12))), 0.02, 0.12)
    vertical_rate = jnp.clip(jnp.exp(jax.random.uniform(seeds[3], (F,), jnp.float32, math.log(0.02), math.log(0.12))), 0.02, 0.12)
    centres = draw_centres(jax.random.fold_in(jax.random.fold_in(seeds[6], part), 71), part)
    slot_storm = jax.random.permutation(own_keys[5], NESTS).astype(jnp.int32)
    return dict(parent_field=parent_field, nest_fields=nest_fields, lateral_rate=lateral_rate, vertical_rate=vertical_rate, centres=centres, slot_storm=slot_storm)


def tendency(field, lateral_rate, vertical_rate):
    padded = jnp.pad(field, ((0, 0), (1, 1), (1, 1), (1, 1)))
    centre = padded[:, 1:-1, 1:-1, 1:-1]
    lateral = padded[:, 1:-1, 2:, 1:-1] + padded[:, 1:-1, :-2, 1:-1] + padded[:, 1:-1, 1:-1, 2:] + padded[:, 1:-1, 1:-1, :-2] - 4.0 * centre
    upright = padded[:, 2:, 1:-1, 1:-1] + padded[:, :-2, 1:-1, 1:-1] - 2.0 * centre
    return lateral_rate[:, None, None, None] * lateral + vertical_rate[:, None, None, None] * upright


def zone_weights():
    nest_span = 3 * FP
    indices = jnp.arange(nest_span, dtype=jnp.int32)
    edge_gap = jnp.minimum(indices, nest_span - 1 - indices)
    distance = jnp.minimum(edge_gap[:, None], edge_gap[None, :])
    weight = jnp.maximum(3 * BWP - distance, 0).astype(jnp.float32) / jnp.float32(3 * BWP)
    inside = (distance >= 1).astype(jnp.float32)
    return weight, inside


def reference(parent_field, nest_fields, lateral_rate, vertical_rate, centres, slot_storm):
    weight, inside = zone_weights()
    nest_span = 3 * FP
    margin = 3 * MOVE
    zero_index = jnp.zeros((), jnp.int32)
    parent_now = parent_field
    nests_now = nest_fields
    for step_index in range(STEPS):
        parent_now = parent_now + tendency(parent_now, lateral_rate, vertical_rate)
        later_pos = centres[step_index + 1][slot_storm]
        before = centres[step_index][slot_storm]
        anchor = (later_pos - FP // 2).astype(jnp.int32)
        offsets = (3 * (later_pos - before)).astype(jnp.int32)
        current = parent_now

        def advance(inputs):
            nest_state, corner, offset = inputs
            window = lax.dynamic_slice(current, (zero_index, zero_index, corner[0], corner[1]), (F, LEV, FP, FP))
            fine_values = jnp.repeat(jnp.repeat(window, 3, axis=2), 3, axis=3)
            padded = jnp.pad(nest_state, ((0, 0), (0, 0), (margin, margin), (margin, margin)))
            shifted = lax.dynamic_slice(padded, (zero_index, zero_index, margin + offset[0], margin + offset[1]), (F, LEV, nest_span, nest_span))
            indices = jnp.arange(nest_span, dtype=jnp.int32)
            row_source = indices + offset[0]
            col_source = indices + offset[1]
            keep_mask = ((row_source >= 0) & (row_source < nest_span))[:, None] & ((col_source >= 0) & (col_source < nest_span))[None, :]
            retained = jnp.where(keep_mask, shifted, fine_values)
            relaxed = retained + weight * (fine_values - retained)
            return relaxed + inside * tendency(relaxed, lateral_rate, vertical_rate)

        nests_now = lax.map(advance, (nests_now, anchor, offsets))
    return parent_now, nests_now
```

```python
import functools
import jax
import jax.numpy as jnp
from jax import lax
from jax.experimental import pallas as pl
from jax.experimental.pallas import tpu as pltpu
from jax.sharding import PartitionSpec as P

FP = 128
BWP = 2
MOVE = 2
HALO = 16
LANES = 128
ALONG = 72
SPAN = 3 * FP
BORDER = 3 * BWP
GROUP = ("tile", "nest", "lev")
EXACT = lax.Precision.HIGHEST


def extended(cells, sides, width):
    for axis, dim in sides:
        count = lax.axis_size(axis)
        ends = count - 1
        head = lax.slice_in_dim(cells, 0, width, axis=dim)
        tail = lax.slice_in_dim(cells, cells.shape[dim] - width, cells.shape[dim], axis=dim)
        cells = jnp.concatenate(
            [
                lax.ppermute(tail, axis, [(i, (i + 1) % count) for i in range(ends)]),
                cells,
                lax.ppermute(head, axis, [((i + 1) % count, i) for i in range(ends)]),
            ],
            axis=dim,
        )
    return cells


def advanced(padded, lateral_rate, vertical_rate):
    padded = jnp.pad(padded, ((0, 0), (1, 1), (0, 0), (0, 0)))
    centre = padded[:, 1:-1, 1:-1, 1:-1]
    lateral = (
        padded[:, 1:-1, 2:, 1:-1]
        + padded[:, 1:-1, :-2, 1:-1]
        + padded[:, 1:-1, 1:-1, 2:]
        + padded[:, 1:-1, 1:-1, :-2]
        - 4.0 * centre
    )
    upright = padded[:, 2:, 1:-1, 1:-1] + padded[:, :-2, 1:-1, 1:-1] - 2.0 * centre
    return (
        centre
        + lateral_rate[:, None, None, None] * lateral
        + vertical_rate[:, None, None, None] * upright
    )


def select_rows(picker, table):
    return jnp.sum(picker[:, :, None] * table[None, :, :], axis=1)


def scatter_kernel(counts, x_ref, y_ref, slots, send_sem, recv_sem):
    tiles, nests, levs = counts
    total = tiles * nests * levs
    me = (lax.axis_index("tile") * nests + lax.axis_index("nest")) * levs + lax.axis_index("lev")

    def partner(k):
        other = lax.rem(me + k, total)
        return other, {
            "tile": other // (nests * levs),
            "nest": lax.rem(other // levs, nests),
            "lev": lax.rem(other, levs),
        }

    def copy(k):
        other, place = partner(k)
        return pltpu.make_async_remote_copy(
            src_ref=x_ref.at[other],
            dst_ref=slots.at[k],
            send_sem=send_sem.at[k],
            recv_sem=recv_sem.at[k],
            device_id=place,
            device_id_type=pl.DeviceIdType.MESH,
        )

    barrier = pltpu.get_barrier_semaphore()

    def greet(k, carry):
        pl.semaphore_signal(
            barrier, inc=1, device_id=partner(k)[1], device_id_type=pl.DeviceIdType.MESH
        )
        return carry

    lax.fori_loop(1, total, greet, 0)
    pl.semaphore_wait(barrier, total - 1)

    def begin(k, carry):
        copy(k).start()
        return carry

    lax.fori_loop(1, total, begin, 0)
    y_ref[...] = x_ref[me]

    def finish(k, carry):
        copy(k).wait()
        y_ref[...] += slots[k]
        return carry

    lax.fori_loop(1, total, finish, 0)


def scatter_sum(terms, counts):
    total, rows, lanes = terms.shape
    return pl.pallas_call(
        functools.partial(scatter_kernel, counts),
        out_shape=jax.ShapeDtypeStruct((rows, lanes), jnp.float32),
        in_specs=[pl.BlockSpec(memory_space=pltpu.VMEM)],
        out_specs=pl.BlockSpec(memory_space=pltpu.VMEM),
        scratch_shapes=[
            pltpu.VMEM((total, rows, lanes), jnp.float32),
            pltpu.SemaphoreType.DMA((total,)),
            pltpu.SemaphoreType.DMA((total,)),
        ],
        compiler_params=pltpu.CompilerParams(
            collective_id=0, has_side_effects=True, vmem_limit_bytes=48 * 1024 * 1024
        ),
    )(terms)


def nest_kernel(rows, cols, steps, offs, place, lateral, vertical, x_ref, sn_ref, we_ref, o_ref):
    slot = pl.program_id(0)
    field = pl.program_id(1)
    slots = pl.num_programs(0)
    high, wide = x_ref.shape[3], x_ref.shape[4]
    rate_l = lateral[field]
    rate_v = vertical[field]
    r = lax.broadcasted_iota(jnp.int32, (high, wide), 0) + (place[0] * rows - HALO)
    j = lax.broadcasted_iota(jnp.int32, (high, wide), 1)
    c = j + place[1] * jnp.where(j >= cols, cols - wide, cols)
    gap_r = jnp.minimum(r, SPAN - 1 - r)
    gap_c = jnp.minimum(c, SPAN - 1 - c)
    gap = jnp.minimum(gap_r, gap_c)
    weight = jnp.maximum(BORDER - gap, 0).astype(jnp.float32) / jnp.float32(BORDER)
    inside = gap >= 1
    near_row = gap_r < BORDER
    second_row = ((r >= 3) & (r < BORDER)) | (r >= SPAN - 3)
    second_col = ((c >= 3) & (c < BORDER)) | (c >= SPAN - 3)
    state = [x_ref[0, 0, 0], x_ref[0, 0, 1]]
    for step in range(steps):
        at = (step * slots + slot) * 2
        down = offs[at]
        right = offs[at + 1]
        keep = (r + down >= 0) & (r + down < SPAN) & (c + right >= 0) & (c + right < SPAN)
        turn_r = lax.rem(high - down, high)
        turn_c = lax.rem(wide - right, wide)
        relaxed = []
        for v in range(2):
            k = 2 * step
            along = jnp.where(second_row, sn_ref[0, 0, v, k + 1 : k + 2, :], sn_ref[0, 0, v, k : k + 1, :])
            across = jnp.where(second_col, we_ref[0, 0, v, :, k + 1 : k + 2], we_ref[0, 0, v, :, k : k + 1])
            driving = jnp.where(near_row, along, across)
            moved = pltpu.roll(pltpu.roll(state[v], turn_r, 0), turn_c, 1)
            retained = jnp.where(keep, moved, driving)
            relaxed.append(retained + weight * (driving - retained))
        for v in range(2):
            here = relaxed[v]
            around = (
                pltpu.roll(here, 1, 0)
                + pltpu.roll(here, high - 1, 0)
                + pltpu.roll(here, 1, 1)
                + pltpu.roll(here, wide - 1, 1)
                - 4.0 * here
            )
            change = rate_l * around + rate_v * (relaxed[1 - v] - 2.0 * here)
            state[v] = jnp.where(inside, here + change, here)
    for v in range(2):
        o_ref[0, 0, v] = state[v][HALO : HALO + rows, :cols]


def advance_nests(wide_nests, along, across, offs, place, lateral, vertical, rows, cols, steps):
    slots, fields, levels, high, wide = wide_nests.shape
    spec = lambda *tail: pl.BlockSpec((1, 1) + tail, lambda n, f, *_: (n, f, 0, 0, 0))
    return pl.pallas_call(
        functools.partial(nest_kernel, rows, cols, steps),
        out_shape=jax.ShapeDtypeStruct((slots, fields, levels, rows, cols), jnp.float32),
        grid_spec=pltpu.PrefetchScalarGridSpec(
            num_scalar_prefetch=4,
            grid=(slots, fields),
            in_specs=[
                spec(levels, high, wide),
                spec(levels, 2 * steps, wide),
                spec(levels, high, 2 * steps),
            ],
            out_specs=spec(levels, rows, cols),
        ),
        compiler_params=pltpu.CompilerParams(vmem_limit_bytes=32 * 1024 * 1024),
    )(offs, place, lateral, vertical, wide_nests, along, across)


def per_device(parent_field, nest_fields, lateral_rate, vertical_rate, centres, slot_storm):
    fields, levels, prow, pcol = parent_field.shape
    slots, _, _, rows, cols = nest_fields.shape
    storms = slot_storm.shape[0]
    steps = centres.shape[0] - 1
    tiles = lax.axis_size("tile")
    groups = lax.axis_size("nest")
    levs = lax.axis_size("lev")
    tile_at = lax.axis_index("tile")
    nest_at = lax.axis_index("nest")
    lev_at = lax.axis_index("lev")
    coarse = rows // 3
    assert levs == 2 and tiles > 1 and steps == 2 and levels == 2
    total = tiles * groups * levs

    nearer = jnp.where(lev_at == 0, nest_fields[..., LANES:cols], nest_fields[..., : cols - LANES])
    other = lax.ppermute(nearer, "lev", [(0, 1), (1, 0)])
    wide_nests = jnp.concatenate([nest_fields, other], axis=4)
    wide_nests = extended(wide_nests, (("tile", 3),), HALO)
    wide = wide_nests.shape[4]
    high = wide_nests.shape[3]

    padded = extended(parent_field, (("tile", 2), (("nest", "lev"), 3)), steps)
    first = advanced(padded, lateral_rate, vertical_rate)
    xg = tile_at * prow + jnp.arange(prow, dtype=jnp.int32)
    yg = (nest_at * levs + lev_at) * pcol + jnp.arange(pcol, dtype=jnp.int32)
    xw = tile_at * prow - 1 + jnp.arange(prow + 2, dtype=jnp.int32)
    yw = (nest_at * levs + lev_at) * pcol - 1 + jnp.arange(pcol + 2, dtype=jnp.int32)
    fine_x = (xw >= 0) & (xw < prow * tiles)
    fine_y = (yw >= 0) & (yw < pcol * groups * levs)
    first = jnp.where(fine_x[:, None] & fine_y[None, :], first, 0.0)
    second = advanced(first, lateral_rate, vertical_rate)
    stages = (first[:, :, 1:-1, 1:-1], second)

    storm_ids = jnp.arange(storms, dtype=jnp.int32)
    pick = (slot_storm[:, None] == storm_ids[None, :]).astype(jnp.int32)
    place_at = [select_rows(pick, centres[n]) for n in range(steps + 1)]
    offs = jnp.stack([3 * (place_at[n + 1] - place_at[n]) for n in range(steps)])
    offs = lax.dynamic_slice_in_dim(offs, nest_at * slots, slots, 1).reshape(-1)

    edges = jnp.array([0, 1, FP - 2, FP - 1], jnp.int32)
    lane = jnp.arange(LANES, dtype=jnp.int32)
    starts = jnp.array([0, FP - ALONG], jnp.int32)
    along_at = jnp.where(lane < ALONG, starts[:, None] + lane[None, :], -SPAN * SPAN)
    rows_at = (jnp.arange(tiles, dtype=jnp.int32) * coarse - 4 - ALONG)[:, None] + lane[None, :]
    rows_at = jnp.where((lane >= ALONG) & (rows_at >= 0) & (rows_at < FP), rows_at, -SPAN * SPAN)
    parts = []
    for n in range(steps):
        now = stages[n].reshape(fields * levels, prow, pcol)
        corner = place_at[n + 1] - FP // 2
        row_edge = (corner[:, 0, None, None] + edges[None, :, None] == xg).astype(jnp.float32)
        col_edge = (corner[:, 1, None, None] + edges[None, :, None] == yg).astype(jnp.float32)
        col_pick = (corner[:, 1, None, None, None] + along_at[None, None] == yg[None, :, None, None])
        row_pick = (corner[:, 0, None, None, None] + rows_at[None, None] == xg[None, :, None, None])
        col_pick = col_pick.astype(jnp.float32).reshape(storms, pcol, levs * LANES)
        row_pick = row_pick.astype(jnp.float32).reshape(storms, prow, tiles * LANES)
        sn = jnp.einsum("jrx,fxy->jrfy", row_edge, now, precision=EXACT)
        sn = jnp.einsum("jrfy,jyc->jrfc", sn, col_pick, precision=EXACT)
        we = jnp.einsum("jky,fxy->jkfx", col_edge, now, precision=EXACT)
        we = jnp.einsum("jkfx,jxc->jkfc", we, row_pick, precision=EXACT)
        sn = sn.reshape(groups, slots, 2, 2, fields * levels, levs, LANES)
        we = we.reshape(groups, slots, 2, 2, fields * levels, tiles, LANES)
        sn_low = jnp.moveaxis(sn[:, :, 0], 4, 1)
        sn_high = jnp.moveaxis(sn[:, :, 1], 4, 1)
        we = jnp.transpose(we, (5, 0, 2, 1, 3, 4, 6))
        parts.append(
            jnp.concatenate(
                [(we[0] + sn_low)[None], we[1:-1], (we[-1] + sn_high)[None]], axis=0
            )
        )
    terms = jnp.stack(parts, axis=4)
    terms = terms.reshape(total, slots * steps * 2 * fields * levels, LANES)
    zone = scatter_sum(terms, (tiles, groups, levs))
    zone = zone.reshape(slots, 2 * steps, fields, levels, LANES)

    jj = jnp.arange(wide, dtype=jnp.int32)
    col_cell = jj + lev_at * jnp.where(jj >= cols, cols - wide, cols)
    row_cell = tile_at * rows - HALO + jnp.arange(high, dtype=jnp.int32)
    spread_c = (lane[:, None] < ALONG) & (col_cell // 3 - lev_at * (FP - ALONG) == lane[:, None])
    spread_r = (lane[:, None] >= ALONG) & (
        row_cell // 3 - (tile_at * coarse - 4 - ALONG) == lane[:, None]
    )
    along = jnp.einsum("nkfvl,lc->nfvkc", zone, spread_c.astype(jnp.float32), precision=EXACT)
    across = jnp.einsum("nkfvl,lr->nfvrk", zone, spread_r.astype(jnp.float32), precision=EXACT)
    place = jnp.stack([tile_at, lev_at]).astype(jnp.int32)
    nests = advance_nests(
        wide_nests, along, across, offs, place, lateral_rate, vertical_rate, rows, cols, steps
    )
    return (second, nests)


def solution(mesh):
    placed = (
        P("member", None, "tile", ("nest", "lev")),
        P(("member", "nest"), None, None, "tile", "lev"),
        P(),
        P(),
        P("member", None, None),
        P("member"),
    )
    return jax.shard_map(
        per_device,
        mesh=mesh,
        in_specs=placed,
        out_specs=(
            P("member", None, "tile", ("nest", "lev")),
            P(("member", "nest"), None, None, "tile", "lev"),
        ),
        check_vma=False,
    )
```

```python
import functools
import jax
import jax.numpy as jnp
from jax import lax
from jax.experimental import pallas as pl
from jax.experimental.pallas import tpu as pltpu
from jax.sharding import PartitionSpec as P

FP = 128
BWP = 2
MOVE = 2
HALO = 16
LANES = 128
ALONG = 72
SPAN = 3 * FP
BORDER = 3 * BWP
EXACT = lax.Precision.HIGHEST


def select_rows(picker, table):
    return jnp.sum(picker[:, :, None] * table[None, :, :], axis=1)


MESH = pl.DeviceIdType.MESH


def halo_kernel(counts, p_ref, n_ref, lat_ref, ver_ref, one_ref, two_ref, w_ref,
                field, side, pack, held, cols_out, cols_in, send, recv):
    tiles, groups, levs = counts
    tile_at = lax.axis_index("tile")
    nest_at = lax.axis_index("nest")
    lev_at = lax.axis_index("lev")
    planes, prow, pcol = p_ref.shape
    blocks, rows, cols = n_ref.shape
    half = cols - LANES
    edge = 8
    above = tile_at > 0
    below = tile_at < tiles - 1
    beyond = ((lev_at == 0) & (nest_at > 0)) | ((lev_at == 1) & (nest_at < groups - 1))
    step_out = 2 * lev_at - 1
    sibling = {"lev": 1 - lev_at}
    outer = {"nest": jnp.clip(nest_at + step_out, 0, groups - 1), "lev": 1 - lev_at}
    upper = {"tile": jnp.maximum(tile_at - 1, 0)}
    lower = {"tile": jnp.minimum(tile_at + 1, tiles - 1)}

    def remote(src, dst, at, landing, place):
        return pltpu.make_async_remote_copy(
            src_ref=src,
            dst_ref=dst,
            send_sem=send.at[at],
            recv_sem=recv.at[landing],
            device_id=place,
            device_id_type=MESH,
        )

    barrier = pltpu.get_barrier_semaphore()

    def greet(place):
        pl.semaphore_signal(barrier, inc=1, device_id=place, device_id_type=MESH)

    greet(sibling)
    pl.when(above)(lambda: greet(upper))
    pl.when(below)(lambda: greet(lower))
    pl.when(beyond)(lambda: greet(outer))
    pl.semaphore_wait(
        barrier,
        1 + above.astype(jnp.int32) + below.astype(jnp.int32) + beyond.astype(jnp.int32),
    )

    rows_up = remote(p_ref.at[:, pl.ds(0, edge)], field.at[:, pl.ds(prow + edge, edge)], 0, 0, upper)
    rows_down = remote(p_ref.at[:, pl.ds(prow - edge, edge)], field.at[:, pl.ds(0, edge)], 1, 1, lower)
    pl.when(above)(rows_up.start)
    pl.when(below)(rows_down.start)

    def gather(i, carry):
        def nearer(b):
            return jnp.where(lev_at == 0, n_ref[b, :, LANES:], n_ref[b, :, :half])

        pack[i] = jnp.concatenate([nearer(2 * i), nearer(2 * i + 1)], axis=1)
        return carry

    lax.fori_loop(0, blocks // 2, gather, 0)
    across = remote(pack, held, 4, 4, sibling)
    across.start()

    field[:, edge : edge + prow, :] = p_ref[...]

    @pl.when(jnp.logical_not(above))
    def _():
        field[:, :edge, :] = jnp.zeros((planes, edge, pcol), jnp.float32)

    @pl.when(jnp.logical_not(below))
    def _():
        field[:, prow + edge :, :] = jnp.zeros((planes, edge, pcol), jnp.float32)

    pl.when(above)(rows_up.wait_send)
    pl.when(below)(rows_down.wait_send)
    pl.when(below)(rows_up.wait_recv)
    pl.when(above)(rows_down.wait_recv)

    tall = prow + 2 * edge
    lane = lax.broadcasted_iota(jnp.int32, (tall, LANES), 1)
    first = jnp.zeros((tall, LANES), jnp.float32)
    last = jnp.zeros((tall, LANES), jnp.float32)
    for f in range(planes):
        mine = (lane == 2 * f) | (lane == 2 * f + 1)
        here = field[f]
        first = jnp.where(mine, pltpu.roll(here, 2 * f, 1) if f else here, first)
        last = jnp.where(mine, pltpu.roll(here, 2 * f + 2, 1), last)
    cols_out[0] = jnp.where(lev_at == 0, last, first)
    cols_out[1] = jnp.where(lev_at == 0, first, last)
    to_sibling = remote(cols_out.at[0], cols_in.at[0], 2, 2, sibling)
    to_outer = remote(cols_out.at[1], cols_in.at[1], 3, 3, outer)
    to_sibling.start()
    pl.when(beyond)(to_outer.start)

    @pl.when(jnp.logical_not(beyond))
    def _():
        cols_in[1] = jnp.zeros((tall, LANES), jnp.float32)

    across.wait()

    def widen(i, carry):
        both = held[i]
        for o in range(2):
            b = 2 * i + o
            w_ref[b, HALO : HALO + rows, :LANES] = n_ref[b, :, :LANES]
            w_ref[b, HALO : HALO + rows, LANES:] = jnp.concatenate(
                [n_ref[b, :, LANES:], both[:, o * half : (o + 1) * half]], axis=1
            )
        return carry

    lax.fori_loop(0, blocks // 2, widen, 0)
    nest_up = remote(w_ref.at[:, pl.ds(HALO, HALO)], w_ref.at[:, pl.ds(HALO + rows, HALO)], 5, 5, upper)
    nest_down = remote(w_ref.at[:, pl.ds(rows, HALO)], w_ref.at[:, pl.ds(0, HALO)], 6, 6, lower)
    pl.when(above)(nest_up.start)
    pl.when(below)(nest_down.start)

    @pl.when(jnp.logical_not(above))
    def _():
        w_ref[:, :HALO, :] = jnp.zeros((blocks, HALO, 2 * LANES), jnp.float32)

    @pl.when(jnp.logical_not(below))
    def _():
        w_ref[:, HALO + rows :, :] = jnp.zeros((blocks, HALO, 2 * LANES), jnp.float32)

    to_sibling.wait()
    pl.when(beyond)(to_outer.wait)
    left = jnp.where(lev_at == 0, cols_in[1], cols_in[0])
    right = jnp.where(lev_at == 0, cols_in[0], cols_in[1])
    for f in range(planes):
        after = pltpu.roll(right, LANES - 2 * f, 1) if f else right
        before = pltpu.roll(left, LANES - 2 - 2 * f, 1)
        side[f] = jnp.where(lane < 2, after, jnp.where(lane >= LANES - 2, before, 0.0))

    wide = 2 * LANES
    x = tile_at * prow - edge + lax.broadcasted_iota(jnp.int32, (tall, wide), 0)
    y = lax.broadcasted_iota(jnp.int32, (tall, wide), 1)
    y = (nest_at * levs + lev_at) * pcol + jnp.where(y >= LANES + 2, y - wide, y)
    domain = (x >= 0) & (x < prow * tiles) & (y >= 0) & (y < pcol * groups * levs)

    def advance(i, carry):
        rate_l = lat_ref[i]
        rate_v = ver_ref[i]
        now = [jnp.concatenate([field[2 * i + v], side[2 * i + v]], axis=1) for v in range(2)]
        for step, out in ((0, one_ref), (1, two_ref)):
            later = []
            for v in range(2):
                here = now[v]
                around = (
                    pltpu.roll(here, 1, 0)
                    + pltpu.roll(here, tall - 1, 0)
                    + pltpu.roll(here, 1, 1)
                    + pltpu.roll(here, wide - 1, 1)
                    - 4.0 * here
                )
                change = rate_l * around + rate_v * (now[1 - v] - 2.0 * here)
                later.append(jnp.where(domain, here + change, 0.0))
            now = later
            for v in range(2):
                out[2 * i + v] = now[v][edge : edge + prow, :pcol]
        return carry

    lax.fori_loop(0, planes // 2, advance, 0)

    pl.when(above)(nest_up.wait_send)
    pl.when(below)(nest_down.wait_send)
    pl.when(below)(nest_up.wait_recv)
    pl.when(above)(nest_down.wait_recv)


def exchange_halos(parent, nests, lateral, vertical, counts):
    planes, prow, pcol = parent.shape
    blocks, rows, cols = nests.shape
    assert pcol == LANES and planes % 2 == 0 and blocks % 2 == 0 and 2 * (cols - LANES) == LANES
    vmem = pl.BlockSpec(memory_space=pltpu.VMEM)
    smem = pl.BlockSpec(memory_space=pltpu.SMEM)
    tall = prow + 16
    shape = lambda *dims: jax.ShapeDtypeStruct(dims, jnp.float32)
    return pl.pallas_call(
        functools.partial(halo_kernel, counts),
        out_shape=(
            shape(planes, prow, pcol),
            shape(planes, prow, pcol),
            shape(blocks, rows + 2 * HALO, 2 * LANES),
        ),
        in_specs=[vmem, vmem, smem, smem],
        out_specs=(vmem, vmem, vmem),
        scratch_shapes=[
            pltpu.VMEM((planes, tall, LANES), jnp.float32),
            pltpu.VMEM((planes, tall, LANES), jnp.float32),
            pltpu.VMEM((blocks // 2, rows, LANES), jnp.float32),
            pltpu.VMEM((blocks // 2, rows, LANES), jnp.float32),
            pltpu.VMEM((2, tall, LANES), jnp.float32),
            pltpu.VMEM((2, tall, LANES), jnp.float32),
            pltpu.SemaphoreType.DMA((7,)),
            pltpu.SemaphoreType.DMA((7,)),
        ],
        compiler_params=pltpu.CompilerParams(
            collective_id=1, has_side_effects=True, vmem_limit_bytes=48 * 1024 * 1024
        ),
    )(parent, nests, lateral, vertical)


def zone_kernel(counts, we_ref, sn_ref, we_out, sn_out, we_sum, sn_sum, we_in, sn_in,
                pair_send, pair_recv, we_send, we_recv, sn_send, sn_recv):
    tiles, groups, levs = counts
    chips = tiles * groups
    tile_at = lax.axis_index("tile")
    nest_at = lax.axis_index("nest")
    lev_at = lax.axis_index("lev")
    me = tile_at * groups + nest_at
    edge = (tile_at == 0) | (tile_at == tiles - 1)
    sibling = {"lev": 1 - lev_at}

    def chip(k):
        other = lax.rem(me + k, chips)
        return other, other // groups, lax.rem(other, groups)

    def we_copy(k):
        other, t, g = chip(k)
        return pltpu.make_async_remote_copy(
            src_ref=we_sum.at[other],
            dst_ref=we_in.at[k],
            send_sem=we_send.at[k],
            recv_sem=we_recv.at[k],
            device_id={"tile": t, "nest": g},
            device_id_type=MESH,
        )

    def sn_copy(k):
        other, t, g = chip(k)
        side = jnp.where(t == 0, 0, 1)
        return pltpu.make_async_remote_copy(
            src_ref=sn_sum.at[side * groups + g],
            dst_ref=sn_in.at[k],
            send_sem=sn_send.at[k],
            recv_sem=sn_recv.at[k],
            device_id={"tile": t, "nest": g},
            device_id_type=MESH,
        )

    def to_edge(k):
        other, t, g = chip(k)
        return (t == 0) | (t == tiles - 1)

    barrier = pltpu.get_barrier_semaphore()
    pl.semaphore_signal(barrier, inc=1, device_id=sibling, device_id_type=MESH)

    def greet(k, carry):
        other, t, g = chip(k)
        pl.semaphore_signal(
            barrier, inc=1, device_id={"tile": t, "nest": g}, device_id_type=MESH
        )
        return carry

    lax.fori_loop(1, chips, greet, 0)
    pl.semaphore_wait(barrier, chips)

    pairs = []
    for at, (src, dst) in enumerate(((sn_ref, sn_sum), (we_ref, we_sum))):
        pair = pltpu.make_async_remote_copy(
            src_ref=src.at[1 - lev_at],
            dst_ref=dst,
            send_sem=pair_send.at[at],
            recv_sem=pair_recv.at[at],
            device_id=sibling,
            device_id_type=MESH,
        )
        pair.start()
        pairs.append(pair)
    pairs[0].wait()
    sn_sum[...] += sn_ref[lev_at]

    def begin_sn(k, carry):
        pl.when(to_edge(k))(lambda: sn_copy(k).start())
        return carry

    lax.fori_loop(1, chips, begin_sn, 0)
    pairs[1].wait()
    we_sum[...] += we_ref[lev_at]

    def begin_we(k, carry):
        we_copy(k).start()
        return carry

    lax.fori_loop(1, chips, begin_we, 0)

    we_out[...] = we_sum[me]
    side_at = jnp.where(tile_at == 0, 0, 1)
    sn_out[...] = sn_sum[side_at * groups + nest_at]

    def finish(k, carry):
        pl.when(to_edge(k))(lambda: sn_copy(k).wait_send())

        @pl.when(edge)
        def _():
            sn_copy(k).wait_recv()
            sn_out[...] += sn_in[k]

        we_copy(k).wait()
        we_out[...] += we_in[k]
        return carry

    lax.fori_loop(1, chips, finish, 0)


def sum_zones(we, sn, counts):
    tiles, groups, levs = counts
    chips = tiles * groups
    vmem = pl.BlockSpec(memory_space=pltpu.VMEM)
    return pl.pallas_call(
        functools.partial(zone_kernel, counts),
        out_shape=(
            jax.ShapeDtypeStruct(we.shape[2:], jnp.float32),
            jax.ShapeDtypeStruct(sn.shape[2:], jnp.float32),
        ),
        in_specs=[vmem, vmem],
        out_specs=(vmem, vmem),
        scratch_shapes=[
            pltpu.VMEM(we.shape[1:], jnp.float32),
            pltpu.VMEM(sn.shape[1:], jnp.float32),
            pltpu.VMEM((chips,) + we.shape[2:], jnp.float32),
            pltpu.VMEM((chips,) + sn.shape[2:], jnp.float32),
            pltpu.SemaphoreType.DMA((2,)),
            pltpu.SemaphoreType.DMA((2,)),
            pltpu.SemaphoreType.DMA((chips,)),
            pltpu.SemaphoreType.DMA((chips,)),
            pltpu.SemaphoreType.DMA((chips,)),
            pltpu.SemaphoreType.DMA((chips,)),
        ],
        compiler_params=pltpu.CompilerParams(
            collective_id=0, has_side_effects=True, vmem_limit_bytes=48 * 1024 * 1024
        ),
    )(we, sn)


def nest_kernel(rows, cols, steps, offs, place, lateral, vertical, x_ref, sn_ref, we_ref, o_ref):
    slot = pl.program_id(0)
    field = pl.program_id(1)
    slots = pl.num_programs(0)
    high, wide = x_ref.shape[3], x_ref.shape[4]
    rate_l = lateral[field]
    rate_v = vertical[field]
    r = lax.broadcasted_iota(jnp.int32, (high, wide), 0) + (place[0] * rows - HALO)
    j = lax.broadcasted_iota(jnp.int32, (high, wide), 1)
    c = j + place[1] * jnp.where(j >= cols, cols - wide, cols)
    gap_r = jnp.minimum(r, SPAN - 1 - r)
    gap_c = jnp.minimum(c, SPAN - 1 - c)
    gap = jnp.minimum(gap_r, gap_c)
    weight = jnp.maximum(BORDER - gap, 0).astype(jnp.float32) / jnp.float32(BORDER)
    inside = gap >= 1
    near_row = gap_r < BORDER
    second_row = ((r >= 3) & (r < BORDER)) | (r >= SPAN - 3)
    second_col = ((c >= 3) & (c < BORDER)) | (c >= SPAN - 3)
    state = [x_ref[0, 0, 0], x_ref[0, 0, 1]]
    for step in range(steps):
        at = (step * slots + slot) * 2
        down = offs[at]
        right = offs[at + 1]
        keep = (r + down >= 0) & (r + down < SPAN) & (c + right >= 0) & (c + right < SPAN)
        turn_r = lax.rem(high - down, high)
        turn_c = lax.rem(wide - right, wide)
        relaxed = []
        for v in range(2):
            k = 2 * step
            along = jnp.where(second_row, sn_ref[0, 0, v, k + 1 : k + 2, :], sn_ref[0, 0, v, k : k + 1, :])
            across = jnp.where(second_col, we_ref[0, 0, v, :, k + 1 : k + 2], we_ref[0, 0, v, :, k : k + 1])
            driving = jnp.where(near_row, along, across)
            moved = pltpu.roll(pltpu.roll(state[v], turn_r, 0), turn_c, 1)
            retained = jnp.where(keep, moved, driving)
            relaxed.append(retained + weight * (driving - retained))
        for v in range(2):
            here = relaxed[v]
            around = (
                pltpu.roll(here, 1, 0)
                + pltpu.roll(here, high - 1, 0)
                + pltpu.roll(here, 1, 1)
                + pltpu.roll(here, wide - 1, 1)
                - 4.0 * here
            )
            change = rate_l * around + rate_v * (relaxed[1 - v] - 2.0 * here)
            state[v] = jnp.where(inside, here + change, here)
    for v in range(2):
        o_ref[0, 0, v] = state[v][HALO : HALO + rows, :cols]


def advance_nests(wide_nests, along, across, offs, place, lateral, vertical, rows, cols, steps):
    slots, fields, levels, high, wide = wide_nests.shape
    spec = lambda *tail: pl.BlockSpec((1, 1) + tail, lambda n, f, *_: (n, f, 0, 0, 0))
    return pl.pallas_call(
        functools.partial(nest_kernel, rows, cols, steps),
        out_shape=jax.ShapeDtypeStruct((slots, fields, levels, rows, cols), jnp.float32),
        grid_spec=pltpu.PrefetchScalarGridSpec(
            num_scalar_prefetch=4,
            grid=(slots, fields),
            in_specs=[
                spec(levels, high, wide),
                spec(levels, 2 * steps, wide),
                spec(levels, high, 2 * steps),
            ],
            out_specs=spec(levels, rows, cols),
        ),
        compiler_params=pltpu.CompilerParams(vmem_limit_bytes=32 * 1024 * 1024),
    )(offs, place, lateral, vertical, wide_nests, along, across)


def per_device(parent_field, nest_fields, lateral_rate, vertical_rate, centres, slot_storm):
    fields, levels, prow, pcol = parent_field.shape
    slots, _, _, rows, cols = nest_fields.shape
    storms = slot_storm.shape[0]
    steps = centres.shape[0] - 1
    tiles = lax.axis_size("tile")
    groups = lax.axis_size("nest")
    levs = lax.axis_size("lev")
    tile_at = lax.axis_index("tile")
    nest_at = lax.axis_index("nest")
    lev_at = lax.axis_index("lev")
    coarse = rows // 3
    assert levs == 2 and tiles > 1 and steps == 2 and levels == 2

    counts = (tiles, groups, levs)
    planes = fields * levels
    first, second, wide_nests = exchange_halos(
        parent_field.reshape(planes, prow, pcol),
        nest_fields.reshape(slots * planes, rows, cols),
        lateral_rate,
        vertical_rate,
        counts,
    )
    high, wide = wide_nests.shape[1:]
    wide_nests = wide_nests.reshape(slots, fields, levels, high, wide)
    stages = (first, second)
    xg = tile_at * prow + jnp.arange(prow, dtype=jnp.int32)
    yg = (nest_at * levs + lev_at) * pcol + jnp.arange(pcol, dtype=jnp.int32)

    storm_ids = jnp.arange(storms, dtype=jnp.int32)
    pick = (slot_storm[:, None] == storm_ids[None, :]).astype(jnp.int32)
    place_at = [select_rows(pick, centres[n]) for n in range(steps + 1)]
    offs = jnp.stack([3 * (place_at[n + 1] - place_at[n]) for n in range(steps)])
    offs = lax.dynamic_slice_in_dim(offs, nest_at * slots, slots, 1).reshape(-1)

    edges = jnp.array([0, 1, FP - 2, FP - 1], jnp.int32)
    deep = coarse + 8
    rows_at = (jnp.arange(tiles, dtype=jnp.int32) * coarse - 4)[:, None] + jnp.arange(deep, dtype=jnp.int32)
    rows_at = jnp.where((rows_at >= 0) & (rows_at < FP), rows_at, -SPAN * SPAN)
    lanes = -(-slots * ALONG // LANES) * LANES
    lane = jnp.arange(lanes, dtype=jnp.int32)
    starts = jnp.array([0, FP - ALONG], jnp.int32)
    along_at = starts[None, :, None] + lane - ALONG * jnp.arange(slots, dtype=jnp.int32)[:, None, None]
    own_lane = lane // ALONG == jnp.arange(slots, dtype=jnp.int32)[:, None, None]
    along_at = jnp.where(own_lane, along_at, -SPAN * SPAN)
    sn_parts = []
    we_parts = []
    for n in range(steps):
        now = stages[n]
        corner = place_at[n + 1] - FP // 2
        row_edge = (corner[:, 0, None, None] + edges[None, :, None] == xg).astype(jnp.float32)
        col_edge = (corner[:, 1, None, None] + edges[None, :, None] == yg).astype(jnp.float32)
        col_at = corner[:, 1].reshape(groups, slots, 1, 1, 1) + along_at[None, :, :, None, :]
        col_pick = (col_at == yg[:, None]).astype(jnp.float32)
        row_pick = (corner[:, 0, None, None, None] + rows_at[None, :, :, None] == xg).astype(jnp.float32)
        sn = jnp.einsum("jrx,fxy->jrfy", row_edge, now, precision=EXACT)
        sn = sn.reshape(groups, slots, 2, 2, planes, pcol)
        sn_parts.append(jnp.einsum("gnhkfy,gnlyc->lhgkfc", sn, col_pick, precision=EXACT))
        we = jnp.einsum("jky,fxy->jkfx", col_edge, now, precision=EXACT)
        we = jnp.einsum("jtrx,jkfx->jtrkf", row_pick, we, precision=EXACT)
        we_parts.append(we.reshape(groups, slots, tiles, deep, levs, 2, planes))
    sn = jnp.stack(sn_parts, axis=3).reshape(levs, 2 * groups, steps * 2 * planes, lanes)
    we = jnp.stack(we_parts, axis=0)
    we = jnp.transpose(we, (5, 3, 1, 4, 2, 6, 0, 7))
    we = we.reshape(levs, tiles * groups, deep, slots * 2 * steps * planes)
    we = jnp.pad(we, ((0, 0), (0, 0), (0, 0), (0, -we.shape[3] % LANES)))
    we, sn = sum_zones(we, sn, counts)

    jj = jnp.arange(wide, dtype=jnp.int32)
    col_cell = jj + lev_at * jnp.where(jj >= cols, cols - wide, cols)
    row_cell = tile_at * rows - HALO + jnp.arange(high, dtype=jnp.int32)
    from_col = col_cell // 3 - lev_at * (FP - ALONG)
    spread_c = (own_lane[:, 0, :, None] & (from_col == (lane % ALONG)[:, None])).astype(jnp.float32)
    from_row = row_cell // 3 - (tile_at * coarse - 4)
    spread_r = (from_row[:, None] == jnp.arange(deep, dtype=jnp.int32)).astype(jnp.float32)
    along = jnp.einsum("ql,nlc->nqc", sn, spread_c, precision=EXACT)
    along = along.reshape(slots, 2 * steps, fields, levels, wide)
    along = jnp.transpose(along, (0, 2, 3, 1, 4))
    across = jnp.einsum("rq,qm->rm", spread_r, we, precision=EXACT)
    across = across[:, : slots * 2 * steps * planes].reshape(high, slots, 2, steps, fields, levels)
    across = jnp.transpose(across, (1, 4, 5, 0, 3, 2)).reshape(slots, fields, levels, high, 2 * steps)
    place = jnp.stack([tile_at, lev_at]).astype(jnp.int32)
    nests = advance_nests(
        wide_nests, along, across, offs, place, lateral_rate, vertical_rate, rows, cols, steps
    )
    return (second.reshape(parent_field.shape), nests)


def solution(mesh):
    placed = (
        P("member", None, "tile", ("nest", "lev")),
        P(("member", "nest"), None, None, "tile", "lev"),
        P(),
        P(),
        P("member", None, None),
        P("member"),
    )
    return jax.shard_map(
        per_device,
        mesh=mesh,
        in_specs=placed,
        out_specs=(
            P("member", None, "tile", ("nest", "lev")),
            P(("member", "nest"), None, None, "tile", "lev"),
        ),
        check_vma=False,
    )
```

```python
import functools
import jax
import jax.numpy as jnp
from jax import lax
from jax.experimental import pallas as pl
from jax.experimental.pallas import tpu as pltpu
from jax.sharding import PartitionSpec as P

FP = 128
BWP = 2
MOVE = 2
HALO = 16
LANES = 128
ALONG = 72
SPAN = 3 * FP
BORDER = 3 * BWP
EXACT = lax.Precision.HIGHEST


MESH = pl.DeviceIdType.MESH


def halo_kernel(counts, p_hbm, n_hbm, lat_ref, ver_ref, stage_ref, w_ref,
                p_ref, n_ref, load, field, side, pack, held, cols_out, cols_in, send, recv):
    tiles, groups, levs = counts
    tile_at = lax.axis_index("tile")
    nest_at = lax.axis_index("nest")
    lev_at = lax.axis_index("lev")
    planes, prow, pcol = p_ref.shape
    blocks, rows, cols = n_ref.shape
    half = cols - LANES
    edge = 8
    above = tile_at > 0
    below = tile_at < tiles - 1
    beyond = ((lev_at == 0) & (nest_at > 0)) | ((lev_at == 1) & (nest_at < groups - 1))
    step_out = 2 * lev_at - 1
    sibling = {"lev": 1 - lev_at}
    outer = {"nest": jnp.clip(nest_at + step_out, 0, groups - 1), "lev": 1 - lev_at}
    upper = {"tile": jnp.maximum(tile_at - 1, 0)}
    lower = {"tile": jnp.minimum(tile_at + 1, tiles - 1)}

    def remote(src, dst, at, landing, place):
        return pltpu.make_async_remote_copy(
            src_ref=src,
            dst_ref=dst,
            send_sem=send.at[at],
            recv_sem=recv.at[landing],
            device_id=place,
            device_id_type=MESH,
        )

    load_parent = pltpu.make_async_copy(p_hbm, p_ref, load.at[0])
    load_nests = pltpu.make_async_copy(n_hbm, n_ref, load.at[1])
    load_parent.start()
    load_nests.start()
    barrier = pltpu.get_barrier_semaphore()

    def greet(place):
        pl.semaphore_signal(barrier, inc=1, device_id=place, device_id_type=MESH)

    greet(sibling)
    pl.when(above)(lambda: greet(upper))
    pl.when(below)(lambda: greet(lower))
    pl.when(beyond)(lambda: greet(outer))
    pl.semaphore_wait(
        barrier,
        1 + above.astype(jnp.int32) + below.astype(jnp.int32) + beyond.astype(jnp.int32),
    )

    load_parent.wait()
    rows_up = remote(p_ref.at[:, pl.ds(0, edge)], field.at[:, pl.ds(prow + edge, edge)], 0, 0, upper)
    rows_down = remote(p_ref.at[:, pl.ds(prow - edge, edge)], field.at[:, pl.ds(0, edge)], 1, 1, lower)
    pl.when(above)(rows_up.start)
    pl.when(below)(rows_down.start)

    load_nests.wait()

    def gather(i, carry):
        def nearer(b):
            return jnp.where(lev_at == 0, n_ref[b, :, LANES:], n_ref[b, :, :half])

        pack[i] = jnp.concatenate([nearer(2 * i), nearer(2 * i + 1)], axis=1)
        return carry

    lax.fori_loop(0, blocks // 2, gather, 0)
    across = remote(pack, held, 4, 4, sibling)
    across.start()

    field[:, edge : edge + prow, :] = p_ref[...]

    @pl.when(jnp.logical_not(above))
    def _():
        field[:, :edge, :] = jnp.zeros((planes, edge, pcol), jnp.float32)

    @pl.when(jnp.logical_not(below))
    def _():
        field[:, prow + edge :, :] = jnp.zeros((planes, edge, pcol), jnp.float32)

    pl.when(above)(rows_up.wait_send)
    pl.when(below)(rows_down.wait_send)
    pl.when(below)(rows_up.wait_recv)
    pl.when(above)(rows_down.wait_recv)

    tall = prow + 2 * edge
    lane = lax.broadcasted_iota(jnp.int32, (tall, LANES), 1)
    first = jnp.zeros((tall, LANES), jnp.float32)
    last = jnp.zeros((tall, LANES), jnp.float32)
    for f in range(planes):
        mine = (lane == 2 * f) | (lane == 2 * f + 1)
        here = field[f]
        first = jnp.where(mine, pltpu.roll(here, 2 * f, 1) if f else here, first)
        last = jnp.where(mine, pltpu.roll(here, 2 * f + 2, 1), last)
    cols_out[0] = jnp.where(lev_at == 0, last, first)
    cols_out[1] = jnp.where(lev_at == 0, first, last)
    to_sibling = remote(cols_out.at[0], cols_in.at[0], 2, 2, sibling)
    to_outer = remote(cols_out.at[1], cols_in.at[1], 3, 3, outer)
    to_sibling.start()
    pl.when(beyond)(to_outer.start)

    @pl.when(jnp.logical_not(beyond))
    def _():
        cols_in[1] = jnp.zeros((tall, LANES), jnp.float32)

    across.wait()

    def widen(i, carry):
        both = held[i]
        for o in range(2):
            b = 2 * i + o
            whole = n_ref[b, :, :LANES]
            mixed = jnp.concatenate([n_ref[b, :, LANES:], both[:, o * half : (o + 1) * half]], axis=1)
            w_ref[b, 0, HALO : HALO + rows, :] = jnp.where(lev_at == 0, whole, mixed)
            w_ref[b, 1, HALO : HALO + rows, :] = jnp.where(lev_at == 0, mixed, whole)
        return carry

    lax.fori_loop(0, blocks // 2, widen, 0)
    nest_up = remote(
        w_ref.at[:, :, pl.ds(HALO, HALO)], w_ref.at[:, :, pl.ds(HALO + rows, HALO)], 5, 5, upper
    )
    nest_down = remote(w_ref.at[:, :, pl.ds(rows, HALO)], w_ref.at[:, :, pl.ds(0, HALO)], 6, 6, lower)
    pl.when(above)(nest_up.start)
    pl.when(below)(nest_down.start)

    @pl.when(jnp.logical_not(above))
    def _():
        w_ref[:, :, :HALO, :] = jnp.zeros((blocks, 2, HALO, LANES), jnp.float32)

    @pl.when(jnp.logical_not(below))
    def _():
        w_ref[:, :, HALO + rows :, :] = jnp.zeros((blocks, 2, HALO, LANES), jnp.float32)

    to_sibling.wait()
    pl.when(beyond)(to_outer.wait)
    left = jnp.where(lev_at == 0, cols_in[1], cols_in[0])
    right = jnp.where(lev_at == 0, cols_in[0], cols_in[1])
    for f in range(planes):
        after = pltpu.roll(right, LANES - 2 * f, 1) if f else right
        before = pltpu.roll(left, LANES - 2 - 2 * f, 1)
        side[f] = jnp.where(lane < 2, after, jnp.where(lane >= LANES - 2, before, 0.0))

    wide = 2 * LANES
    x = tile_at * prow - edge + lax.broadcasted_iota(jnp.int32, (tall, wide), 0)
    y = lax.broadcasted_iota(jnp.int32, (tall, wide), 1)
    y = (nest_at * levs + lev_at) * pcol + jnp.where(y >= LANES + 2, y - wide, y)
    domain = (x >= 0) & (x < prow * tiles) & (y >= 0) & (y < pcol * groups * levs)

    def advance(i, carry):
        rate_l = lat_ref[i]
        rate_v = ver_ref[i]
        now = [jnp.concatenate([field[2 * i + v], side[2 * i + v]], axis=1) for v in range(2)]
        for step in range(2):
            later = []
            for v in range(2):
                here = now[v]
                around = (
                    pltpu.roll(here, 1, 0)
                    + pltpu.roll(here, tall - 1, 0)
                    + pltpu.roll(here, 1, 1)
                    + pltpu.roll(here, wide - 1, 1)
                    - 4.0 * here
                )
                change = rate_l * around + rate_v * (now[1 - v] - 2.0 * here)
                later.append(jnp.where(domain, here + change, 0.0))
            now = later
            for v in range(2):
                stage_ref[step, 2 * i + v] = now[v][edge : edge + prow, :pcol]
        return carry

    lax.fori_loop(0, planes // 2, advance, 0)

    pl.when(above)(nest_up.wait_send)
    pl.when(below)(nest_down.wait_send)
    pl.when(below)(nest_up.wait_recv)
    pl.when(above)(nest_down.wait_recv)


def exchange_halos(parent, nests, lateral, vertical, counts):
    planes, prow, pcol = parent.shape
    blocks, rows, cols = nests.shape
    assert pcol == LANES and planes % 2 == 0 and blocks % 2 == 0 and 2 * (cols - LANES) == LANES
    vmem = pl.BlockSpec(memory_space=pltpu.VMEM)
    smem = pl.BlockSpec(memory_space=pltpu.SMEM)
    anywhere = pl.BlockSpec(memory_space=pl.ANY)
    tall = prow + 16
    shape = lambda *dims: jax.ShapeDtypeStruct(dims, jnp.float32)
    return pl.pallas_call(
        functools.partial(halo_kernel, counts),
        out_shape=(
            shape(2, planes, prow, pcol),
            shape(blocks, 2, rows + 2 * HALO, LANES),
        ),
        in_specs=[anywhere, anywhere, smem, smem],
        out_specs=(vmem, vmem),
        scratch_shapes=[
            pltpu.VMEM((planes, prow, pcol), jnp.float32),
            pltpu.VMEM((blocks, rows, cols), jnp.float32),
            pltpu.SemaphoreType.DMA((2,)),
            pltpu.VMEM((planes, tall, LANES), jnp.float32),
            pltpu.VMEM((planes, tall, LANES), jnp.float32),
            pltpu.VMEM((blocks // 2, rows, LANES), jnp.float32),
            pltpu.VMEM((blocks // 2, rows, LANES), jnp.float32),
            pltpu.VMEM((2, tall, LANES), jnp.float32),
            pltpu.VMEM((2, tall, LANES), jnp.float32),
            pltpu.SemaphoreType.DMA((7,)),
            pltpu.SemaphoreType.DMA((7,)),
        ],
        compiler_params=pltpu.CompilerParams(
            collective_id=1, has_side_effects=True, vmem_limit_bytes=24 * 1024 * 1024
        ),
    )(parent, nests, lateral, vertical)


def zone_kernel(counts, we_ref, sn_ref, we_out, sn_out, we_sum, sn_sum, we_in, sn_in,
                pair_send, pair_recv, we_send, we_recv, sn_send, sn_recv):
    tiles, groups, levs = counts
    chips = tiles * groups
    tile_at = lax.axis_index("tile")
    nest_at = lax.axis_index("nest")
    lev_at = lax.axis_index("lev")
    me = tile_at * groups + nest_at
    edge = (tile_at == 0) | (tile_at == tiles - 1)
    sibling = {"lev": 1 - lev_at}

    def chip(k):
        other = lax.rem(me + k, chips)
        return other, other // groups, lax.rem(other, groups)

    def we_copy(k):
        other, t, g = chip(k)
        return pltpu.make_async_remote_copy(
            src_ref=we_sum.at[other],
            dst_ref=we_in.at[k],
            send_sem=we_send.at[k],
            recv_sem=we_recv.at[k],
            device_id={"tile": t, "nest": g},
            device_id_type=MESH,
        )

    def sn_copy(k):
        other, t, g = chip(k)
        side = jnp.where(t == 0, 0, 1)
        return pltpu.make_async_remote_copy(
            src_ref=sn_sum.at[side * groups + g],
            dst_ref=sn_in.at[k],
            send_sem=sn_send.at[k],
            recv_sem=sn_recv.at[k],
            device_id={"tile": t, "nest": g},
            device_id_type=MESH,
        )

    def to_edge(k):
        other, t, g = chip(k)
        return (t == 0) | (t == tiles - 1)

    barrier = pltpu.get_barrier_semaphore()
    pl.semaphore_signal(barrier, inc=1, device_id=sibling, device_id_type=MESH)

    def greet(k, carry):
        other, t, g = chip(k)
        pl.semaphore_signal(
            barrier, inc=1, device_id={"tile": t, "nest": g}, device_id_type=MESH
        )
        return carry

    lax.fori_loop(1, chips, greet, 0)
    pl.semaphore_wait(barrier, chips)

    pairs = []
    for at, (src, dst) in enumerate(((sn_ref, sn_sum), (we_ref, we_sum))):
        pair = pltpu.make_async_remote_copy(
            src_ref=src.at[1 - lev_at],
            dst_ref=dst,
            send_sem=pair_send.at[at],
            recv_sem=pair_recv.at[at],
            device_id=sibling,
            device_id_type=MESH,
        )
        pair.start()
        pairs.append(pair)
    pairs[0].wait()
    sn_sum[...] += sn_ref[lev_at]

    def begin_sn(k, carry):
        pl.when(to_edge(k))(lambda: sn_copy(k).start())
        return carry

    lax.fori_loop(1, chips, begin_sn, 0)
    pairs[1].wait()
    we_sum[...] += we_ref[lev_at]

    def begin_we(k, carry):
        we_copy(k).start()
        return carry

    lax.fori_loop(1, chips, begin_we, 0)

    we_out[...] = we_sum[me]
    side_at = jnp.where(tile_at == 0, 0, 1)
    sn_out[...] = sn_sum[side_at * groups + nest_at]

    def finish(k, carry):
        pl.when(to_edge(k))(lambda: sn_copy(k).wait_send())

        @pl.when(edge)
        def _():
            sn_copy(k).wait_recv()
            sn_out[...] += sn_in[k]

        we_copy(k).wait()
        we_out[...] += we_in[k]
        return carry

    lax.fori_loop(1, chips, finish, 0)


def sum_zones(we, sn, counts):
    tiles, groups, levs = counts
    chips = tiles * groups
    room = 8 * 1024 * 1024 + 4 * sum(a.size * (2 * levs + 2) for a in (we, sn)) // levs
    vmem = pl.BlockSpec(memory_space=pltpu.VMEM)
    return pl.pallas_call(
        functools.partial(zone_kernel, counts),
        out_shape=(
            jax.ShapeDtypeStruct(we.shape[2:], jnp.float32),
            jax.ShapeDtypeStruct(sn.shape[2:], jnp.float32),
        ),
        in_specs=[vmem, vmem],
        out_specs=(vmem, vmem),
        scratch_shapes=[
            pltpu.VMEM(we.shape[1:], jnp.float32),
            pltpu.VMEM(sn.shape[1:], jnp.float32),
            pltpu.VMEM((chips,) + we.shape[2:], jnp.float32),
            pltpu.VMEM((chips,) + sn.shape[2:], jnp.float32),
            pltpu.SemaphoreType.DMA((2,)),
            pltpu.SemaphoreType.DMA((2,)),
            pltpu.SemaphoreType.DMA((chips,)),
            pltpu.SemaphoreType.DMA((chips,)),
            pltpu.SemaphoreType.DMA((chips,)),
            pltpu.SemaphoreType.DMA((chips,)),
        ],
        compiler_params=pltpu.CompilerParams(
            collective_id=0, has_side_effects=True, vmem_limit_bytes=room
        ),
    )(we, sn)


def nest_kernel(shape, steps, offs, place, lateral, vertical, x_ref, sn_ref, we_ref, o_hbm,
                relaxed, state, done, col_mix, row_mix, sem):
    slots, fields, levels, rows, cols = shape
    high = x_ref.shape[2]
    edge = 8
    mid = high - 2 * edge
    tile_at = place[0]
    lev_at = place[1]
    half = cols - LANES
    lane = lax.broadcasted_iota(jnp.int32, (mid, LANES), 1)
    row = lax.broadcasted_iota(jnp.int32, (mid, LANES), 0) + (tile_at * rows - HALO + edge)
    near = jnp.where(
        lev_at == 0, lane, jnp.where(lane < half, cols + LANES + lane, cols - LANES + lane)
    )
    far = jnp.where(lev_at == 0, LANES, cols) + lane
    col_lane = jnp.where(lev_at == 0, 0, half - 1)
    blocks = (HALO - edge, HALO - edge + rows - edge)

    def mixing(r, c, down, right):
        gap = jnp.minimum(jnp.minimum(r, SPAN - 1 - r), jnp.minimum(c, SPAN - 1 - c))
        weight = jnp.maximum(BORDER - gap, 0).astype(jnp.float32) / jnp.float32(BORDER)
        keep = (r + down >= 0) & (r + down < SPAN) & (c + right >= 0) & (c + right < SPAN)
        return jnp.where(keep, weight, 1.0)

    for n in range(slots):
        shifts = []
        for step in range(steps):
            down = offs[(step * slots + n) * 2]
            right = offs[(step * slots + n) * 2 + 1]
            shifts.append((down, right))
            weight = mixing(row, near, down, right)
            side_row = (row < BORDER) | (row >= SPAN - BORDER)
            gap_c = jnp.minimum(near, SPAN - 1 - near)
            weight = jnp.where(side_row | (gap_c >= BORDER), 0.0, weight)
            second = ((near >= 3) & (near < BORDER)) | (near >= SPAN - 3)
            col_mix[step, 0] = 1.0 - weight
            col_mix[step, 1] = jnp.where(second, 0.0, weight)
            col_mix[step, 2] = jnp.where(second, weight, 0.0)
            for side in range(2):
                for at, start in enumerate(blocks):
                    r = row[start : start + edge]
                    c = (near, far)[side][start : start + edge]
                    weight = mixing(r, c, down, right)
                    weight = jnp.where((r < BORDER) | (r >= SPAN - BORDER), weight, 0.0)
                    second = ((r >= 3) & (r < BORDER)) | (r >= SPAN - 3)
                    row_mix[step, side, at, 0] = 1.0 - weight
                    row_mix[step, side, at, 1] = jnp.where(second, 0.0, weight)
                    row_mix[step, side, at, 2] = jnp.where(second, weight, 0.0)

        def one_field(f, carry):
            rate_l = lateral[f]
            rate_v = vertical[f]
            keep_rate = 1.0 - 4.0 * rate_l - 2.0 * rate_v
            for step in range(steps):
                down, right = shifts[step]
                k = 2 * step
                turn = lax.rem(LANES - right, LANES)
                own = (lane + right >= 0) & (lane + right < LANES)
                for v in range(levels):
                    b = (n * fields + f) * levels + v
                    if step == 0:
                        source = [x_ref[b, side, pl.ds(edge + down, mid), :] for side in range(2)]
                    else:
                        source = [state[v, side, pl.ds(edge + down, mid), :] for side in range(2)]
                    turned = [pltpu.roll(a, turn, 1) for a in source]
                    first = jnp.where(own, turned[0], turned[1])
                    first = (
                        col_mix[step, 0] * first
                        + col_mix[step, 1] * we_ref[b, edge : edge + mid, k : k + 1]
                        + col_mix[step, 2] * we_ref[b, edge : edge + mid, k + 1 : k + 2]
                    )
                    relaxed[v, 0, edge : edge + mid] = first
                    relaxed[v, 1, edge : edge + mid] = jnp.where(own, turned[1], turned[0])
                    for side in range(2):
                        wide = slice(side * LANES, (side + 1) * LANES)
                        for at, start in enumerate(blocks):
                            here = slice(edge + start, 2 * edge + start)
                            relaxed[v, side, here] = (
                                row_mix[step, side, at, 0] * relaxed[v, side, here]
                                + row_mix[step, side, at, 1] * sn_ref[b, k : k + 1, wide]
                                + row_mix[step, side, at, 2] * sn_ref[b, k + 1 : k + 2, wide]
                            )
                for v in range(levels):
                    here = [relaxed[v, side, edge : edge + mid] for side in range(2)]
                    west = [pltpu.roll(a, 1, 1) for a in here]
                    east = [pltpu.roll(a, LANES - 1, 1) for a in here]
                    results = []
                    for side in range(2):
                        around = (
                            relaxed[v, side, edge - 1 : edge - 1 + mid]
                            + relaxed[v, side, edge + 1 : edge + 1 + mid]
                            + jnp.where(lane == 0, west[1 - side], west[side])
                            + jnp.where(lane == LANES - 1, east[1 - side], east[side])
                        )
                        new = (
                            keep_rate * here[side]
                            + rate_l * around
                            + rate_v * relaxed[1 - v, side, edge : edge + mid]
                        )
                        if side == 0:
                            new = jnp.where(lane == col_lane, here[side], new)
                        state[v, side, edge : edge + mid] = new
                    for side in range(2):
                        for at, start in enumerate(blocks):
                            r = row[start : start + edge]
                            spot = slice(edge + start, 2 * edge + start)
                            state[v, side, spot] = jnp.where(
                                (r == 0) | (r == SPAN - 1), relaxed[v, side, spot], state[v, side, spot]
                            )
            for v in range(levels):
                near_part = state[v, 0, HALO : HALO + rows]
                far_part = state[v, 1, HALO : HALO + rows]
                done[n, f, v, :, :LANES] = jnp.where(lev_at == 0, near_part, far_part)
                done[n, f, v, :, LANES:] = jnp.where(lev_at == 0, far_part, near_part)[:, :half]
            return carry

        lax.fori_loop(0, fields, one_field, 0)
        pltpu.make_async_copy(done.at[n], o_hbm.at[n], sem.at[n]).start()
    for n in range(slots):
        pltpu.make_async_copy(done.at[n], o_hbm.at[n], sem.at[n]).wait()


def advance_nests(wide_nests, along, across, offs, place, lateral, vertical, shape, steps):
    slots, fields, levels, rows, cols = shape
    high = wide_nests.shape[2]
    vmem = pl.BlockSpec(memory_space=pltpu.VMEM)
    smem = pl.BlockSpec(memory_space=pltpu.SMEM)
    return pl.pallas_call(
        functools.partial(nest_kernel, shape, steps),
        out_shape=jax.ShapeDtypeStruct(shape, jnp.float32),
        in_specs=[smem] * 4 + [vmem] * 3,
        out_specs=pl.BlockSpec(memory_space=pl.ANY),
        scratch_shapes=[
            pltpu.VMEM((levels, 2, high, LANES), jnp.float32),
            pltpu.VMEM((levels, 2, high, LANES), jnp.float32),
            pltpu.VMEM(shape, jnp.float32),
            pltpu.VMEM((steps, 3, high - 16, LANES), jnp.float32),
            pltpu.VMEM((steps, 2, 2, 3, 8, LANES), jnp.float32),
            pltpu.SemaphoreType.DMA((slots,)),
        ],
        compiler_params=pltpu.CompilerParams(vmem_limit_bytes=24 * 1024 * 1024),
    )(offs, place, lateral, vertical, wide_nests, along, across)


def per_device(parent_field, nest_fields, lateral_rate, vertical_rate, centres, slot_storm):
    fields, levels, prow, pcol = parent_field.shape
    slots, _, _, rows, cols = nest_fields.shape
    storms = slot_storm.shape[0]
    steps = centres.shape[0] - 1
    tiles = lax.axis_size("tile")
    groups = lax.axis_size("nest")
    levs = lax.axis_size("lev")
    tile_at = lax.axis_index("tile")
    nest_at = lax.axis_index("nest")
    lev_at = lax.axis_index("lev")
    coarse = rows // 3
    assert levs == 2 and tiles > 1 and steps == 2 and levels == 2

    counts = (tiles, groups, levs)
    planes = fields * levels
    stages, wide_nests = exchange_halos(
        parent_field.reshape(planes, prow, pcol),
        nest_fields.reshape(slots * planes, rows, cols),
        lateral_rate,
        vertical_rate,
        counts,
    )
    high = wide_nests.shape[2]
    wide = 2 * LANES
    xg = tile_at * prow + jnp.arange(prow, dtype=jnp.int32)
    yg = (nest_at * levs + lev_at) * pcol + jnp.arange(pcol, dtype=jnp.int32)

    storm_ids = jnp.arange(storms, dtype=jnp.int32)
    pick = (slot_storm[:, None] == storm_ids[None, :]).astype(jnp.int32)
    place_at = jnp.sum(pick[None, :, :, None] * centres[:, None, :, :], axis=2)
    offs = 3 * (place_at[1:] - place_at[:-1])
    offs = lax.dynamic_slice_in_dim(offs, nest_at * slots, slots, 1).reshape(-1)

    edges = jnp.array([0, 1, FP - 2, FP - 1], jnp.int32)
    deep = coarse + 8
    rows_at = (jnp.arange(tiles, dtype=jnp.int32) * coarse - 4)[:, None] + jnp.arange(deep, dtype=jnp.int32)
    rows_at = jnp.where((rows_at >= 0) & (rows_at < FP), rows_at, -SPAN * SPAN)
    lanes = -(-slots * ALONG // LANES) * LANES
    lane = jnp.arange(lanes, dtype=jnp.int32)
    starts = jnp.array([0, FP - ALONG], jnp.int32)
    along_at = starts[None, :, None] + lane - ALONG * jnp.arange(slots, dtype=jnp.int32)[:, None, None]
    own_lane = lane // ALONG == jnp.arange(slots, dtype=jnp.int32)[:, None, None]
    along_at = jnp.where(own_lane, along_at, -SPAN * SPAN)
    corner = place_at[1:] - FP // 2
    corner_r, corner_c = corner[:, :, 0, None, None], corner[:, :, 1, None, None]
    row_edge = (corner_r + edges[:, None] == xg).astype(jnp.float32)
    col_edge = (corner_c + edges[:, None] == yg).astype(jnp.float32)
    col_at = corner[:, :, 1].reshape(steps, groups, slots, 1, 1, 1) + along_at[:, :, None, :]
    col_pick = (col_at == yg[:, None]).astype(jnp.float32)
    row_pick = (corner_r[..., None] + rows_at[:, :, None] == xg).astype(jnp.float32)
    sn = jnp.einsum("sjrx,sfxy->sjrfy", row_edge, stages, precision=EXACT)
    sn = sn.reshape(steps, groups, slots, 2, 2, planes, pcol)
    sn = jnp.einsum("sgnhkfy,sgnlyc->lhgskfc", sn, col_pick, precision=EXACT)
    sn = sn.reshape(levs, 2 * groups, steps * 2 * planes, lanes)
    we = jnp.einsum("sjky,sfxy->sjkfx", col_edge, stages, precision=EXACT)
    we = jnp.einsum("sjtrx,sjkfx->sjtrkf", row_pick, we, precision=EXACT)
    we = we.reshape(steps, groups, slots, tiles, deep, levs, 2, planes)
    we = jnp.transpose(we, (5, 3, 1, 4, 2, 6, 0, 7))
    we = we.reshape(levs, tiles * groups, deep, slots * 2 * steps * planes)
    we = jnp.pad(we, ((0, 0), (0, 0), (0, 0), (0, -we.shape[3] % LANES)))
    we, sn = sum_zones(we, sn, counts)

    jj = jnp.arange(wide, dtype=jnp.int32)
    swapped = jnp.where(jj < cols - LANES, cols + LANES + jj, cols - LANES + jj)
    swapped = jnp.where(jj < LANES, swapped, cols - LANES + jj)
    col_cell = jnp.where(lev_at == 0, jj, swapped)
    row_cell = tile_at * rows - HALO + jnp.arange(high, dtype=jnp.int32)
    from_col = col_cell // 3 - lev_at * (FP - ALONG)
    spread_c = (own_lane[:, 0, :, None] & (from_col == (lane % ALONG)[:, None])).astype(jnp.float32)
    from_row = row_cell // 3 - (tile_at * coarse - 4)
    spread_r = (from_row[:, None] == jnp.arange(deep, dtype=jnp.int32)).astype(jnp.float32)
    along = jnp.einsum("ql,nlc->nqc", sn, spread_c, precision=EXACT)
    along = along.reshape(slots, 2 * steps, fields, levels, wide)
    along = jnp.transpose(along, (0, 2, 3, 1, 4)).reshape(slots * planes, 2 * steps, wide)
    across = jnp.einsum("rq,qm->rm", spread_r, we, precision=EXACT)
    across = across[:, : slots * 2 * steps * planes].reshape(high, slots, 2, steps, fields, levels)
    across = jnp.transpose(across, (1, 4, 5, 0, 3, 2)).reshape(slots * planes, high, 2 * steps)
    place = jnp.stack([tile_at, lev_at]).astype(jnp.int32)
    nests = advance_nests(
        wide_nests, along, across, offs, place, lateral_rate, vertical_rate, nest_fields.shape, steps
    )
    return (stages[1].reshape(parent_field.shape), nests)


def solution(mesh):
    placed = (
        P("member", None, "tile", ("nest", "lev")),
        P(("member", "nest"), None, None, "tile", "lev"),
        P(),
        P(),
        P("member", None, None),
        P("member"),
    )
    return jax.shard_map(
        per_device,
        mesh=mesh,
        in_specs=placed,
        out_specs=(
            P("member", None, "tile", ("nest", "lev")),
            P(("member", "nest"), None, None, "tile", "lev"),
        ),
        check_vma=False,
    )
```

```python
import functools
import jax
import jax.numpy as jnp
from jax import lax
from jax.experimental import pallas as pl
from jax.experimental.pallas import tpu as pltpu
from jax.sharding import PartitionSpec as P

FP = 128
BWP = 2
MOVE = 2
HALO = 16
LANES = 128
ALONG = 72
SPAN = 3 * FP
BORDER = 3 * BWP
EXACT = lax.Precision.HIGHEST


MESH = pl.DeviceIdType.MESH


def halo_kernel(counts, p_hbm, n_hbm, lat_ref, ver_ref, stage_ref, w_hbm,
                p_ref, n_ref, w_ref, load, field, side, pack, held, cols_out, cols_in, send, recv):
    tiles, groups, levs = counts
    tile_at = lax.axis_index("tile")
    nest_at = lax.axis_index("nest")
    lev_at = lax.axis_index("lev")
    planes, prow, pcol = p_ref.shape
    blocks, rows, cols = n_ref.shape
    half = cols - LANES
    edge = 8
    above = tile_at > 0
    below = tile_at < tiles - 1
    beyond = ((lev_at == 0) & (nest_at > 0)) | ((lev_at == 1) & (nest_at < groups - 1))
    step_out = 2 * lev_at - 1
    sibling = {"lev": 1 - lev_at}
    outer = {"nest": jnp.clip(nest_at + step_out, 0, groups - 1), "lev": 1 - lev_at}
    upper = {"tile": jnp.maximum(tile_at - 1, 0)}
    lower = {"tile": jnp.minimum(tile_at + 1, tiles - 1)}

    def remote(src, dst, at, landing, place):
        return pltpu.make_async_remote_copy(
            src_ref=src,
            dst_ref=dst,
            send_sem=send.at[at],
            recv_sem=recv.at[landing],
            device_id=place,
            device_id_type=MESH,
        )

    load_parent = pltpu.make_async_copy(p_hbm, p_ref, load.at[0])
    load_nests = pltpu.make_async_copy(n_hbm, n_ref, load.at[1])
    load_parent.start()
    load_nests.start()
    barrier = pltpu.get_barrier_semaphore()

    def greet(place):
        pl.semaphore_signal(barrier, inc=1, device_id=place, device_id_type=MESH)

    greet(sibling)
    pl.when(above)(lambda: greet(upper))
    pl.when(below)(lambda: greet(lower))
    pl.when(beyond)(lambda: greet(outer))
    pl.semaphore_wait(
        barrier,
        1 + above.astype(jnp.int32) + below.astype(jnp.int32) + beyond.astype(jnp.int32),
    )

    load_parent.wait()
    rows_up = remote(p_ref.at[:, pl.ds(0, edge)], field.at[:, pl.ds(prow + edge, edge)], 0, 0, upper)
    rows_down = remote(p_ref.at[:, pl.ds(prow - edge, edge)], field.at[:, pl.ds(0, edge)], 1, 1, lower)
    pl.when(above)(rows_up.start)
    pl.when(below)(rows_down.start)

    load_nests.wait()

    def gather(i, carry):
        def nearer(b):
            return jnp.where(lev_at == 0, n_ref[b, :, LANES:], n_ref[b, :, :half])

        pack[i] = jnp.concatenate([nearer(2 * i), nearer(2 * i + 1)], axis=1)
        return carry

    lax.fori_loop(0, blocks // 2, gather, 0)
    across = remote(pack, held, 4, 4, sibling)
    across.start()

    field[:, edge : edge + prow, :] = p_ref[...]

    @pl.when(jnp.logical_not(above))
    def _():
        field[:, :edge, :] = jnp.zeros((planes, edge, pcol), jnp.float32)

    @pl.when(jnp.logical_not(below))
    def _():
        field[:, prow + edge :, :] = jnp.zeros((planes, edge, pcol), jnp.float32)

    pl.when(above)(rows_up.wait_send)
    pl.when(below)(rows_down.wait_send)
    pl.when(below)(rows_up.wait_recv)
    pl.when(above)(rows_down.wait_recv)

    tall = prow + 2 * edge
    lane = lax.broadcasted_iota(jnp.int32, (tall, LANES), 1)
    first = jnp.zeros((tall, LANES), jnp.float32)
    last = jnp.zeros((tall, LANES), jnp.float32)
    for f in range(planes):
        mine = (lane == 2 * f) | (lane == 2 * f + 1)
        here = field[f]
        first = jnp.where(mine, pltpu.roll(here, 2 * f, 1) if f else here, first)
        last = jnp.where(mine, pltpu.roll(here, 2 * f + 2, 1), last)
    cols_out[0] = jnp.where(lev_at == 0, last, first)
    cols_out[1] = jnp.where(lev_at == 0, first, last)
    to_sibling = remote(cols_out.at[0], cols_in.at[0], 2, 2, sibling)
    to_outer = remote(cols_out.at[1], cols_in.at[1], 3, 3, outer)
    to_sibling.start()
    pl.when(beyond)(to_outer.start)

    @pl.when(jnp.logical_not(beyond))
    def _():
        cols_in[1] = jnp.zeros((tall, LANES), jnp.float32)

    across.wait()

    def widen(i, carry):
        both = held[i]
        for o in range(2):
            b = 2 * i + o
            whole = n_ref[b, :, :LANES]
            mixed = jnp.concatenate([n_ref[b, :, LANES:], both[:, o * half : (o + 1) * half]], axis=1)
            w_ref[b, 0, HALO : HALO + rows, :] = jnp.where(lev_at == 0, whole, mixed)
            w_ref[b, 1, HALO : HALO + rows, :] = jnp.where(lev_at == 0, mixed, whole)
        return carry

    lax.fori_loop(0, blocks // 2, widen, 0)
    nest_up = remote(
        w_ref.at[:, :, pl.ds(HALO, HALO)], w_ref.at[:, :, pl.ds(HALO + rows, HALO)], 5, 5, upper
    )
    nest_down = remote(w_ref.at[:, :, pl.ds(rows, HALO)], w_ref.at[:, :, pl.ds(0, HALO)], 6, 6, lower)
    pl.when(above)(nest_up.start)
    pl.when(below)(nest_down.start)

    @pl.when(jnp.logical_not(above))
    def _():
        w_ref[:, :, :HALO, :] = jnp.zeros((blocks, 2, HALO, LANES), jnp.float32)

    @pl.when(jnp.logical_not(below))
    def _():
        w_ref[:, :, HALO + rows :, :] = jnp.zeros((blocks, 2, HALO, LANES), jnp.float32)

    to_sibling.wait()
    pl.when(beyond)(to_outer.wait)
    left = jnp.where(lev_at == 0, cols_in[1], cols_in[0])
    right = jnp.where(lev_at == 0, cols_in[0], cols_in[1])
    for f in range(planes):
        after = pltpu.roll(right, LANES - 2 * f, 1) if f else right
        before = pltpu.roll(left, LANES - 2 - 2 * f, 1)
        side[f] = jnp.where(lane < 2, after, jnp.where(lane >= LANES - 2, before, 0.0))

    wide = 2 * LANES
    x = tile_at * prow - edge + lax.broadcasted_iota(jnp.int32, (tall, wide), 0)
    y = lax.broadcasted_iota(jnp.int32, (tall, wide), 1)
    y = (nest_at * levs + lev_at) * pcol + jnp.where(y >= LANES + 2, y - wide, y)
    domain = (x >= 0) & (x < prow * tiles) & (y >= 0) & (y < pcol * groups * levs)

    def advance(i, carry):
        rate_l = lat_ref[i]
        rate_v = ver_ref[i]
        now = [jnp.concatenate([field[2 * i + v], side[2 * i + v]], axis=1) for v in range(2)]
        for step in range(2):
            later = []
            for v in range(2):
                here = now[v]
                around = (
                    pltpu.roll(here, 1, 0)
                    + pltpu.roll(here, tall - 1, 0)
                    + pltpu.roll(here, 1, 1)
                    + pltpu.roll(here, wide - 1, 1)
                    - 4.0 * here
                )
                change = rate_l * around + rate_v * (now[1 - v] - 2.0 * here)
                later.append(jnp.where(domain, here + change, 0.0))
            now = later
            for v in range(2):
                stage_ref[step, 2 * i + v] = now[v][edge : edge + prow, :pcol]
        return carry

    lax.fori_loop(0, planes // 2, advance, 0)

    def keep(at, start, size):
        return pltpu.make_async_copy(
            w_ref.at[:, :, pl.ds(start, size)], w_hbm.at[:, :, pl.ds(start, size)], load.at[at]
        )

    middle = keep(0, HALO, rows)
    middle.start()
    pl.when(above)(nest_up.wait_send)
    pl.when(below)(nest_down.wait_send)
    pl.when(below)(nest_up.wait_recv)
    pl.when(above)(nest_down.wait_recv)
    head = keep(1, 0, HALO)
    tail = keep(2, HALO + rows, HALO)
    head.start()
    tail.start()
    middle.wait()
    head.wait()
    tail.wait()


def exchange_halos(parent, nests, lateral, vertical, counts):
    planes, prow, pcol = parent.shape
    blocks, rows, cols = nests.shape
    assert pcol == LANES and planes % 2 == 0 and blocks % 2 == 0 and 2 * (cols - LANES) == LANES
    vmem = pl.BlockSpec(memory_space=pltpu.VMEM)
    smem = pl.BlockSpec(memory_space=pltpu.SMEM)
    anywhere = pl.BlockSpec(memory_space=pl.ANY)
    tall = prow + 16
    shape = lambda *dims: jax.ShapeDtypeStruct(dims, jnp.float32)
    return pl.pallas_call(
        functools.partial(halo_kernel, counts),
        out_shape=(
            shape(2, planes, prow, pcol),
            shape(blocks, 2, rows + 2 * HALO, LANES),
        ),
        in_specs=[anywhere, anywhere, smem, smem],
        out_specs=(vmem, anywhere),
        scratch_shapes=[
            pltpu.VMEM((planes, prow, pcol), jnp.float32),
            pltpu.VMEM((blocks, rows, cols), jnp.float32),
            pltpu.VMEM((blocks, 2, rows + 2 * HALO, LANES), jnp.float32),
            pltpu.SemaphoreType.DMA((3,)),
            pltpu.VMEM((planes, tall, LANES), jnp.float32),
            pltpu.VMEM((planes, tall, LANES), jnp.float32),
            pltpu.VMEM((blocks // 2, rows, LANES), jnp.float32),
            pltpu.VMEM((blocks // 2, rows, LANES), jnp.float32),
            pltpu.VMEM((2, tall, LANES), jnp.float32),
            pltpu.VMEM((2, tall, LANES), jnp.float32),
            pltpu.SemaphoreType.DMA((7,)),
            pltpu.SemaphoreType.DMA((7,)),
        ],
        compiler_params=pltpu.CompilerParams(
            collective_id=1, has_side_effects=True, vmem_limit_bytes=56 * 1024 * 1024
        ),
    )(parent, nests, lateral, vertical)


def zone_kernel(counts, we_ref, sn_ref, we_out, sn_out, we_sum, sn_sum, we_in, sn_in,
                pair_send, pair_recv, we_send, we_recv, sn_send, sn_recv):
    tiles, groups, levs = counts
    chips = tiles * groups
    tile_at = lax.axis_index("tile")
    nest_at = lax.axis_index("nest")
    lev_at = lax.axis_index("lev")
    me = tile_at * groups + nest_at
    edge = (tile_at == 0) | (tile_at == tiles - 1)
    sibling = {"lev": 1 - lev_at}

    def chip(k):
        other = lax.rem(me + k, chips)
        return other, other // groups, lax.rem(other, groups)

    def we_copy(k):
        other, t, g = chip(k)
        return pltpu.make_async_remote_copy(
            src_ref=we_sum.at[other],
            dst_ref=we_in.at[k],
            send_sem=we_send.at[k],
            recv_sem=we_recv.at[k],
            device_id={"tile": t, "nest": g},
            device_id_type=MESH,
        )

    def sn_copy(k):
        other, t, g = chip(k)
        side = jnp.where(t == 0, 0, 1)
        return pltpu.make_async_remote_copy(
            src_ref=sn_sum.at[side * groups + g],
            dst_ref=sn_in.at[k],
            send_sem=sn_send.at[k],
            recv_sem=sn_recv.at[k],
            device_id={"tile": t, "nest": g},
            device_id_type=MESH,
        )

    def to_edge(k):
        other, t, g = chip(k)
        return (t == 0) | (t == tiles - 1)

    barrier = pltpu.get_barrier_semaphore()
    pl.semaphore_signal(barrier, inc=1, device_id=sibling, device_id_type=MESH)

    def greet(k, carry):
        other, t, g = chip(k)
        pl.semaphore_signal(
            barrier, inc=1, device_id={"tile": t, "nest": g}, device_id_type=MESH
        )
        return carry

    lax.fori_loop(1, chips, greet, 0)
    pl.semaphore_wait(barrier, chips)

    pairs = []
    for at, (src, dst) in enumerate(((sn_ref, sn_sum), (we_ref, we_sum))):
        pair = pltpu.make_async_remote_copy(
            src_ref=src.at[1 - lev_at],
            dst_ref=dst,
            send_sem=pair_send.at[at],
            recv_sem=pair_recv.at[at],
            device_id=sibling,
            device_id_type=MESH,
        )
        pair.start()
        pairs.append(pair)
    pairs[0].wait()
    sn_sum[...] += sn_ref[lev_at]

    def begin_sn(k, carry):
        pl.when(to_edge(k))(lambda: sn_copy(k).start())
        return carry

    lax.fori_loop(1, chips, begin_sn, 0)
    pairs[1].wait()
    we_sum[...] += we_ref[lev_at]

    def begin_we(k, carry):
        we_copy(k).start()
        return carry

    lax.fori_loop(1, chips, begin_we, 0)

    we_out[...] = we_sum[me]
    side_at = jnp.where(tile_at == 0, 0, 1)
    sn_out[...] = sn_sum[side_at * groups + nest_at]

    def finish(k, carry):
        pl.when(to_edge(k))(lambda: sn_copy(k).wait_send())

        @pl.when(edge)
        def _():
            sn_copy(k).wait_recv()
            sn_out[...] += sn_in[k]

        we_copy(k).wait()
        we_out[...] += we_in[k]
        return carry

    lax.fori_loop(1, chips, finish, 0)


def sum_zones(we, sn, counts):
    tiles, groups, levs = counts
    chips = tiles * groups
    room = 8 * 1024 * 1024 + 4 * sum(a.size * (2 * levs + 2) for a in (we, sn)) // levs
    vmem = pl.BlockSpec(memory_space=pltpu.VMEM)
    return pl.pallas_call(
        functools.partial(zone_kernel, counts),
        out_shape=(
            jax.ShapeDtypeStruct(we.shape[2:], jnp.float32),
            jax.ShapeDtypeStruct(sn.shape[2:], jnp.float32),
        ),
        in_specs=[vmem, vmem],
        out_specs=(vmem, vmem),
        scratch_shapes=[
            pltpu.VMEM(we.shape[1:], jnp.float32),
            pltpu.VMEM(sn.shape[1:], jnp.float32),
            pltpu.VMEM((chips,) + we.shape[2:], jnp.float32),
            pltpu.VMEM((chips,) + sn.shape[2:], jnp.float32),
            pltpu.SemaphoreType.DMA((2,)),
            pltpu.SemaphoreType.DMA((2,)),
            pltpu.SemaphoreType.DMA((chips,)),
            pltpu.SemaphoreType.DMA((chips,)),
            pltpu.SemaphoreType.DMA((chips,)),
            pltpu.SemaphoreType.DMA((chips,)),
        ],
        compiler_params=pltpu.CompilerParams(
            collective_id=0, has_side_effects=True, vmem_limit_bytes=room
        ),
    )(we, sn)


def nest_kernel(shape, steps, offs, place, lateral, vertical, x_hbm, sn_ref, we_ref, o_hbm,
                x_ref, relaxed, state, done, col_mix, row_mix, load, sem):
    slots, fields, levels, rows, cols = shape
    planes = fields * levels
    high = x_ref.shape[2]
    edge = 8
    mid = high - 2 * edge

    def fetch(n):
        part = pl.ds(n * planes, planes)
        return pltpu.make_async_copy(x_hbm.at[part], x_ref.at[part], load.at[n])

    for n in range(slots):
        fetch(n).start()
    tile_at = place[0]
    lev_at = place[1]
    half = cols - LANES
    lane = lax.broadcasted_iota(jnp.int32, (mid, LANES), 1)
    row = lax.broadcasted_iota(jnp.int32, (mid, LANES), 0) + (tile_at * rows - HALO + edge)
    near = jnp.where(
        lev_at == 0, lane, jnp.where(lane < half, cols + LANES + lane, cols - LANES + lane)
    )
    far = jnp.where(lev_at == 0, LANES, cols) + lane
    col_lane = jnp.where(lev_at == 0, 0, half - 1)
    blocks = (HALO - edge, HALO - edge + rows - edge)

    def mixing(r, c, down, right):
        gap = jnp.minimum(jnp.minimum(r, SPAN - 1 - r), jnp.minimum(c, SPAN - 1 - c))
        weight = jnp.maximum(BORDER - gap, 0).astype(jnp.float32) / jnp.float32(BORDER)
        keep = (r + down >= 0) & (r + down < SPAN) & (c + right >= 0) & (c + right < SPAN)
        return jnp.where(keep, weight, 1.0)

    def patched(whole, blend):
        parts = []
        past = 0
        for at, start in enumerate(blocks):
            parts += [whole[past:start], blend(at, start, whole[start : start + edge])]
            past = start + edge
        return jnp.concatenate([a for a in parts + [whole[past:]] if a.shape[0]], axis=0)

    def one_nest(n, carry):
        shifts = []
        for step in range(steps):
            down = offs[(step * slots + n) * 2]
            right = offs[(step * slots + n) * 2 + 1]
            shifts.append((down, right))
            weight = mixing(row, near, down, right)
            side_row = (row < BORDER) | (row >= SPAN - BORDER)
            gap_c = jnp.minimum(near, SPAN - 1 - near)
            weight = jnp.where(side_row | (gap_c >= BORDER), 0.0, weight)
            second = ((near >= 3) & (near < BORDER)) | (near >= SPAN - 3)
            col_mix[step, 0] = 1.0 - weight
            col_mix[step, 1] = jnp.where(second, 0.0, weight)
            col_mix[step, 2] = jnp.where(second, weight, 0.0)
            for side in range(2):
                for at, start in enumerate(blocks):
                    r = row[start : start + edge]
                    c = (near, far)[side][start : start + edge]
                    weight = mixing(r, c, down, right)
                    weight = jnp.where((r < BORDER) | (r >= SPAN - BORDER), weight, 0.0)
                    second = ((r >= 3) & (r < BORDER)) | (r >= SPAN - 3)
                    row_mix[step, side, at, 0] = 1.0 - weight
                    row_mix[step, side, at, 1] = jnp.where(second, 0.0, weight)
                    row_mix[step, side, at, 2] = jnp.where(second, weight, 0.0)

        fetch(n).wait()

        def relax(step, f, v):
            down, right = shifts[step]
            k = 2 * step
            turn = lax.rem(LANES - right, LANES)
            own = (lane + right >= 0) & (lane + right < LANES)
            b = n * planes + f * levels + v
            spot = pl.ds(edge + down, mid)
            if step == 0:
                turned = [pltpu.roll(x_ref[b, side, spot, :], turn, 1) for side in range(2)]
            else:
                turned = [
                    pltpu.roll(state[f * levels + v, side, spot, :], turn, 1) for side in range(2)
                ]
            first = jnp.where(own, turned[0], turned[1])
            first = (
                col_mix[step, 0] * first
                + col_mix[step, 1] * we_ref[b, edge : edge + mid, k : k + 1]
                + col_mix[step, 2] * we_ref[b, edge : edge + mid, k + 1 : k + 2]
            )
            halves = (first, jnp.where(own, turned[1], turned[0]))
            for side in range(2):
                wide = slice(side * LANES, (side + 1) * LANES)

                def blend(at, start, block):
                    return (
                        row_mix[step, side, at, 0] * block
                        + row_mix[step, side, at, 1] * sn_ref[b, k : k + 1, wide]
                        + row_mix[step, side, at, 2] * sn_ref[b, k + 1 : k + 2, wide]
                    )

                relaxed[f * levels + v, side, edge : edge + mid] = patched(halves[side], blend)

        def diffuse(f, v):
            rate_l = lateral[f]
            rate_v = vertical[f]
            keep_rate = 1.0 - 4.0 * rate_l - 2.0 * rate_v
            p = f * levels + v
            here = [relaxed[p, side, edge : edge + mid] for side in range(2)]
            west = [pltpu.roll(a, 1, 1) for a in here]
            east = [pltpu.roll(a, LANES - 1, 1) for a in here]
            for side in range(2):
                around = (
                    relaxed[p, side, edge - 1 : edge - 1 + mid]
                    + relaxed[p, side, edge + 1 : edge + 1 + mid]
                    + jnp.where(lane == 0, west[1 - side], west[side])
                    + jnp.where(lane == LANES - 1, east[1 - side], east[side])
                )
                new = (
                    keep_rate * here[side]
                    + rate_l * around
                    + rate_v * relaxed[f * levels + 1 - v, side, edge : edge + mid]
                )
                if side == 0:
                    new = jnp.where(lane == col_lane, here[0], new)

                def blend(at, start, block):
                    r = row[start : start + edge]
                    before = here[side][start : start + edge]
                    return jnp.where((r == 0) | (r == SPAN - 1), before, block)

                state[p, side, edge : edge + mid] = patched(new, blend)

        for step in range(steps):
            for f in range(fields):
                for v in range(levels):
                    relax(step, f, v)
            for f in range(fields):
                for v in range(levels):
                    diffuse(f, v)
        for f in range(fields):
            for v in range(levels):
                near_part = state[f * levels + v, 0, HALO : HALO + rows]
                far_part = state[f * levels + v, 1, HALO : HALO + rows]
                done[n, f, v, :, :LANES] = jnp.where(lev_at == 0, near_part, far_part)
                done[n, f, v, :, LANES:] = jnp.where(lev_at == 0, far_part, near_part)[:, :half]
        pltpu.make_async_copy(done.at[n], o_hbm.at[n], sem.at[n]).start()
        return carry

    lax.fori_loop(0, slots, one_nest, 0)
    for n in range(slots):
        pltpu.make_async_copy(done.at[n], o_hbm.at[n], sem.at[n]).wait()


def advance_nests(wide_nests, along, across, offs, place, lateral, vertical, shape, steps):
    slots, fields, levels, rows, cols = shape
    high = wide_nests.shape[2]
    vmem = pl.BlockSpec(memory_space=pltpu.VMEM)
    smem = pl.BlockSpec(memory_space=pltpu.SMEM)
    return pl.pallas_call(
        functools.partial(nest_kernel, shape, steps),
        out_shape=jax.ShapeDtypeStruct(shape, jnp.float32),
        in_specs=[smem] * 4 + [pl.BlockSpec(memory_space=pl.ANY)] + [vmem] * 2,
        out_specs=pl.BlockSpec(memory_space=pl.ANY),
        scratch_shapes=[
            pltpu.VMEM(wide_nests.shape, jnp.float32),
            pltpu.VMEM((fields * levels, 2, high, LANES), jnp.float32),
            pltpu.VMEM((fields * levels, 2, high, LANES), jnp.float32),
            pltpu.VMEM(shape, jnp.float32),
            pltpu.VMEM((steps, 3, high - 16, LANES), jnp.float32),
            pltpu.VMEM((steps, 2, 2, 3, 8, LANES), jnp.float32),
            pltpu.SemaphoreType.DMA((slots,)),
            pltpu.SemaphoreType.DMA((slots,)),
        ],
        compiler_params=pltpu.CompilerParams(vmem_limit_bytes=56 * 1024 * 1024),
    )(offs, place, lateral, vertical, wide_nests, along, across)


def per_device(parent_field, nest_fields, lateral_rate, vertical_rate, centres, slot_storm):
    fields, levels, prow, pcol = parent_field.shape
    slots, _, _, rows, cols = nest_fields.shape
    storms = slot_storm.shape[0]
    steps = centres.shape[0] - 1
    tiles = lax.axis_size("tile")
    groups = lax.axis_size("nest")
    levs = lax.axis_size("lev")
    tile_at = lax.axis_index("tile")
    nest_at = lax.axis_index("nest")
    lev_at = lax.axis_index("lev")
    coarse = rows // 3
    assert levs == 2 and tiles > 1 and steps == 2 and levels == 2

    counts = (tiles, groups, levs)
    planes = fields * levels
    stages, wide_nests = exchange_halos(
        parent_field.reshape(planes, prow, pcol),
        nest_fields.reshape(slots * planes, rows, cols),
        lateral_rate,
        vertical_rate,
        counts,
    )
    high = wide_nests.shape[2]
    wide = 2 * LANES
    xg = tile_at * prow + jnp.arange(prow, dtype=jnp.int32)
    yg = (nest_at * levs + lev_at) * pcol + jnp.arange(pcol, dtype=jnp.int32)

    storm_ids = jnp.arange(storms, dtype=jnp.int32)
    pick = (slot_storm[:, None] == storm_ids[None, :]).astype(jnp.int32)
    place_at = jnp.sum(pick[None, :, :, None] * centres[:, None, :, :], axis=2)
    offs = 3 * (place_at[1:] - place_at[:-1])
    offs = lax.dynamic_slice_in_dim(offs, nest_at * slots, slots, 1).reshape(-1)

    edges = jnp.array([0, 1, FP - 2, FP - 1], jnp.int32)
    deep = coarse + 8
    rows_at = (jnp.arange(tiles, dtype=jnp.int32) * coarse - 4)[:, None] + jnp.arange(deep, dtype=jnp.int32)
    rows_at = jnp.where((rows_at >= 0) & (rows_at < FP), rows_at, -SPAN * SPAN)
    lanes = -(-slots * ALONG // LANES) * LANES
    lane = jnp.arange(lanes, dtype=jnp.int32)
    starts = jnp.array([0, FP - ALONG], jnp.int32)
    along_at = starts[None, :, None] + lane - ALONG * jnp.arange(slots, dtype=jnp.int32)[:, None, None]
    own_lane = lane // ALONG == jnp.arange(slots, dtype=jnp.int32)[:, None, None]
    along_at = jnp.where(own_lane, along_at, -SPAN * SPAN)
    corner = place_at[1:] - FP // 2
    corner_r, corner_c = corner[:, :, 0, None, None], corner[:, :, 1, None, None]
    row_edge = (corner_r + edges[:, None] == xg).astype(jnp.float32)
    col_edge = (corner_c + edges[:, None] == yg).astype(jnp.float32)
    col_at = corner[:, :, 1].reshape(steps, groups, slots, 1, 1, 1) + along_at[:, :, None, :]
    col_pick = (col_at == yg[:, None]).astype(jnp.float32)
    row_pick = (corner_r[..., None] + rows_at[:, :, None] == xg).astype(jnp.float32)
    sn = jnp.einsum("sjrx,sfxy->sjrfy", row_edge, stages, precision=EXACT)
    sn = sn.reshape(steps, groups, slots, 2, 2, planes, pcol)
    sn = jnp.einsum("sgnhkfy,sgnlyc->lhgskfc", sn, col_pick, precision=EXACT)
    sn = sn.reshape(levs, 2 * groups, steps * 2 * planes, lanes)
    we = jnp.einsum("sjky,sfxy->sjkfx", col_edge, stages, precision=EXACT)
    we = jnp.einsum("sjtrx,sjkfx->sjtrkf", row_pick, we, precision=EXACT)
    we = we.reshape(steps, groups, slots, tiles, deep, levs, 2, planes)
    we = jnp.transpose(we, (5, 3, 1, 4, 2, 6, 0, 7))
    we = we.reshape(levs, tiles * groups, deep, slots * 2 * steps * planes)
    we = jnp.pad(we, ((0, 0), (0, 0), (0, 0), (0, -we.shape[3] % LANES)))
    we, sn = sum_zones(we, sn, counts)

    jj = jnp.arange(wide, dtype=jnp.int32)
    swapped = jnp.where(jj < cols - LANES, cols + LANES + jj, cols - LANES + jj)
    swapped = jnp.where(jj < LANES, swapped, cols - LANES + jj)
    col_cell = jnp.where(lev_at == 0, jj, swapped)
    row_cell = tile_at * rows - HALO + jnp.arange(high, dtype=jnp.int32)
    from_col = col_cell // 3 - lev_at * (FP - ALONG)
    spread_c = (own_lane[:, 0, :, None] & (from_col == (lane % ALONG)[:, None])).astype(jnp.float32)
    from_row = row_cell // 3 - (tile_at * coarse - 4)
    spread_r = (from_row[:, None] == jnp.arange(deep, dtype=jnp.int32)).astype(jnp.float32)
    along = jnp.einsum("ql,nlc->nqc", sn, spread_c, precision=EXACT)
    along = along.reshape(slots, 2 * steps, fields, levels, wide)
    along = jnp.transpose(along, (0, 2, 3, 1, 4)).reshape(slots * planes, 2 * steps, wide)
    across = jnp.einsum("rq,qm->rm", spread_r, we, precision=EXACT)
    across = across[:, : slots * 2 * steps * planes].reshape(high, slots, 2, steps, fields, levels)
    across = jnp.transpose(across, (1, 4, 5, 0, 3, 2)).reshape(slots * planes, high, 2 * steps)
    place = jnp.stack([tile_at, lev_at]).astype(jnp.int32)
    nests = advance_nests(
        wide_nests, along, across, offs, place, lateral_rate, vertical_rate, nest_fields.shape, steps
    )
    return (stages[1].reshape(parent_field.shape), nests)


def solution(mesh):
    placed = (
        P("member", None, "tile", ("nest", "lev")),
        P(("member", "nest"), None, None, "tile", "lev"),
        P(),
        P(),
        P("member", None, None),
        P("member"),
    )
    return jax.shard_map(
        per_device,
        mesh=mesh,
        in_specs=placed,
        out_specs=(
            P("member", None, "tile", ("nest", "lev")),
            P(("member", "nest"), None, None, "tile", "lev"),
        ),
        check_vma=False,
    )
```

```python
import functools
import jax
import jax.numpy as jnp
from jax import lax
from jax.experimental import pallas as pl
from jax.experimental.pallas import tpu as pltpu
from jax.sharding import PartitionSpec as P

FP = 128
BWP = 2
MOVE = 2
HALO = 16
LANES = 128
ALONG = 72
SPAN = 3 * FP
BORDER = 3 * BWP
EXACT = lax.Precision.HIGHEST


MESH = pl.DeviceIdType.MESH


def halo_kernel(counts, p_hbm, n_hbm, lat_ref, ver_ref, stage_ref, w_hbm,
                p_ref, n_ref, w_ref, load, field, side, pack, held, cols_out, cols_in, send, recv):
    tiles, groups, levs = counts
    tile_at = lax.axis_index("tile")
    nest_at = lax.axis_index("nest")
    lev_at = lax.axis_index("lev")
    planes, prow, pcol = p_ref.shape
    blocks, rows, cols = n_ref.shape
    half = cols - LANES
    edge = 8
    above = tile_at > 0
    below = tile_at < tiles - 1
    beyond = ((lev_at == 0) & (nest_at > 0)) | ((lev_at == 1) & (nest_at < groups - 1))
    step_out = 2 * lev_at - 1
    sibling = {"lev": 1 - lev_at}
    outer = {"nest": jnp.clip(nest_at + step_out, 0, groups - 1), "lev": 1 - lev_at}
    upper = {"tile": jnp.maximum(tile_at - 1, 0)}
    lower = {"tile": jnp.minimum(tile_at + 1, tiles - 1)}

    def remote(src, dst, at, landing, place):
        return pltpu.make_async_remote_copy(
            src_ref=src,
            dst_ref=dst,
            send_sem=send.at[at],
            recv_sem=recv.at[landing],
            device_id=place,
            device_id_type=MESH,
        )

    load_parent = pltpu.make_async_copy(p_hbm, p_ref, load.at[0])
    load_nests = pltpu.make_async_copy(n_hbm, n_ref, load.at[1])
    load_parent.start()
    load_nests.start()
    barrier = pltpu.get_barrier_semaphore()

    def greet(place):
        pl.semaphore_signal(barrier, inc=1, device_id=place, device_id_type=MESH)

    greet(sibling)
    pl.when(above)(lambda: greet(upper))
    pl.when(below)(lambda: greet(lower))
    pl.when(beyond)(lambda: greet(outer))
    pl.semaphore_wait(
        barrier,
        1 + above.astype(jnp.int32) + below.astype(jnp.int32) + beyond.astype(jnp.int32),
    )

    load_parent.wait()
    rows_up = remote(p_ref.at[:, pl.ds(0, edge)], field.at[:, pl.ds(prow + edge, edge)], 0, 0, upper)
    rows_down = remote(p_ref.at[:, pl.ds(prow - edge, edge)], field.at[:, pl.ds(0, edge)], 1, 1, lower)
    pl.when(above)(rows_up.start)
    pl.when(below)(rows_down.start)

    load_nests.wait()
    own_up = remote(
        n_ref.at[:, pl.ds(0, HALO), pl.ds(0, LANES)],
        w_ref.at[:, lev_at, pl.ds(HALO + rows, HALO)],
        7, 7, upper,
    )
    own_down = remote(
        n_ref.at[:, pl.ds(rows - HALO, HALO), pl.ds(0, LANES)],
        w_ref.at[:, lev_at, pl.ds(0, HALO)],
        8, 8, lower,
    )
    pl.when(above)(own_up.start)
    pl.when(below)(own_down.start)

    def gather(i, carry):
        def nearer(b):
            return jnp.where(lev_at == 0, n_ref[b, :, LANES:], n_ref[b, :, :half])

        pack[i] = jnp.concatenate([nearer(2 * i), nearer(2 * i + 1)], axis=1)
        return carry

    lax.fori_loop(0, blocks // 2, gather, 0)
    across = remote(pack, held, 4, 4, sibling)
    across.start()

    field[:, edge : edge + prow, :] = p_ref[...]

    @pl.when(jnp.logical_not(above))
    def _():
        field[:, :edge, :] = jnp.zeros((planes, edge, pcol), jnp.float32)

    @pl.when(jnp.logical_not(below))
    def _():
        field[:, prow + edge :, :] = jnp.zeros((planes, edge, pcol), jnp.float32)

    pl.when(above)(rows_up.wait_send)
    pl.when(below)(rows_down.wait_send)
    pl.when(below)(rows_up.wait_recv)
    pl.when(above)(rows_down.wait_recv)

    tall = prow + 2 * edge
    lane = lax.broadcasted_iota(jnp.int32, (tall, LANES), 1)
    first = jnp.zeros((tall, LANES), jnp.float32)
    last = jnp.zeros((tall, LANES), jnp.float32)
    for f in range(planes):
        mine = (lane == 2 * f) | (lane == 2 * f + 1)
        here = field[f]
        first = jnp.where(mine, pltpu.roll(here, 2 * f, 1) if f else here, first)
        last = jnp.where(mine, pltpu.roll(here, 2 * f + 2, 1), last)
    cols_out[0] = jnp.where(lev_at == 0, last, first)
    cols_out[1] = jnp.where(lev_at == 0, first, last)
    to_sibling = remote(cols_out.at[0], cols_in.at[0], 2, 2, sibling)
    to_outer = remote(cols_out.at[1], cols_in.at[1], 3, 3, outer)
    to_sibling.start()
    pl.when(beyond)(to_outer.start)

    @pl.when(jnp.logical_not(beyond))
    def _():
        cols_in[1] = jnp.zeros((tall, LANES), jnp.float32)

    across.wait()

    def widen(i, carry):
        both = held[i]
        for o in range(2):
            b = 2 * i + o
            whole = n_ref[b, :, :LANES]
            mixed = jnp.concatenate([n_ref[b, :, LANES:], both[:, o * half : (o + 1) * half]], axis=1)
            w_ref[b, 0, HALO : HALO + rows, :] = jnp.where(lev_at == 0, whole, mixed)
            w_ref[b, 1, HALO : HALO + rows, :] = jnp.where(lev_at == 0, mixed, whole)
        return carry

    lax.fori_loop(0, blocks // 2, widen, 0)
    mixed_at = 1 - lev_at
    nest_up = remote(
        w_ref.at[:, mixed_at, pl.ds(HALO, HALO)],
        w_ref.at[:, mixed_at, pl.ds(HALO + rows, HALO)],
        5, 5, upper,
    )
    nest_down = remote(
        w_ref.at[:, mixed_at, pl.ds(rows, HALO)], w_ref.at[:, mixed_at, pl.ds(0, HALO)], 6, 6, lower
    )
    pl.when(above)(nest_up.start)
    pl.when(below)(nest_down.start)

    @pl.when(jnp.logical_not(above))
    def _():
        w_ref[:, :, :HALO, :] = jnp.zeros((blocks, 2, HALO, LANES), jnp.float32)

    @pl.when(jnp.logical_not(below))
    def _():
        w_ref[:, :, HALO + rows :, :] = jnp.zeros((blocks, 2, HALO, LANES), jnp.float32)

    to_sibling.wait()
    pl.when(beyond)(to_outer.wait)
    left = jnp.where(lev_at == 0, cols_in[1], cols_in[0])
    right = jnp.where(lev_at == 0, cols_in[0], cols_in[1])
    for f in range(planes):
        after = pltpu.roll(right, LANES - 2 * f, 1) if f else right
        before = pltpu.roll(left, LANES - 2 - 2 * f, 1)
        side[f] = jnp.where(lane < 2, after, jnp.where(lane >= LANES - 2, before, 0.0))

    wide = 2 * LANES
    x = tile_at * prow - edge + lax.broadcasted_iota(jnp.int32, (tall, wide), 0)
    y = lax.broadcasted_iota(jnp.int32, (tall, wide), 1)
    y = (nest_at * levs + lev_at) * pcol + jnp.where(y >= LANES + 2, y - wide, y)
    domain = (x >= 0) & (x < prow * tiles) & (y >= 0) & (y < pcol * groups * levs)

    def advance(i, carry):
        rate_l = lat_ref[i]
        rate_v = ver_ref[i]
        now = [jnp.concatenate([field[2 * i + v], side[2 * i + v]], axis=1) for v in range(2)]
        for step in range(2):
            later = []
            for v in range(2):
                here = now[v]
                around = (
                    pltpu.roll(here, 1, 0)
                    + pltpu.roll(here, tall - 1, 0)
                    + pltpu.roll(here, 1, 1)
                    + pltpu.roll(here, wide - 1, 1)
                    - 4.0 * here
                )
                change = rate_l * around + rate_v * (now[1 - v] - 2.0 * here)
                later.append(jnp.where(domain, here + change, 0.0))
            now = later
            for v in range(2):
                stage_ref[step, 2 * i + v] = now[v][edge : edge + prow, :pcol]
        return carry

    lax.fori_loop(0, planes // 2, advance, 0)

    def keep(at, start, size):
        return pltpu.make_async_copy(
            w_ref.at[:, :, pl.ds(start, size)], w_hbm.at[:, :, pl.ds(start, size)], load.at[at]
        )

    middle = keep(0, HALO, rows)
    middle.start()
    for up, down in ((own_up, own_down), (nest_up, nest_down)):
        pl.when(above)(up.wait_send)
        pl.when(below)(down.wait_send)
        pl.when(below)(up.wait_recv)
        pl.when(above)(down.wait_recv)
    head = keep(1, 0, HALO)
    tail = keep(2, HALO + rows, HALO)
    head.start()
    tail.start()
    middle.wait()
    head.wait()
    tail.wait()


def exchange_halos(parent, nests, lateral, vertical, counts):
    planes, prow, pcol = parent.shape
    blocks, rows, cols = nests.shape
    assert pcol == LANES and planes % 2 == 0 and blocks % 2 == 0 and 2 * (cols - LANES) == LANES
    vmem = pl.BlockSpec(memory_space=pltpu.VMEM)
    smem = pl.BlockSpec(memory_space=pltpu.SMEM)
    anywhere = pl.BlockSpec(memory_space=pl.ANY)
    tall = prow + 16
    shape = lambda *dims: jax.ShapeDtypeStruct(dims, jnp.float32)
    return pl.pallas_call(
        functools.partial(halo_kernel, counts),
        out_shape=(
            shape(2, planes, prow, pcol),
            shape(blocks, 2, rows + 2 * HALO, LANES),
        ),
        in_specs=[anywhere, anywhere, smem, smem],
        out_specs=(vmem, anywhere),
        scratch_shapes=[
            pltpu.VMEM((planes, prow, pcol), jnp.float32),
            pltpu.VMEM((blocks, rows, cols), jnp.float32),
            pltpu.VMEM((blocks, 2, rows + 2 * HALO, LANES), jnp.float32),
            pltpu.SemaphoreType.DMA((3,)),
            pltpu.VMEM((planes, tall, LANES), jnp.float32),
            pltpu.VMEM((planes, tall, LANES), jnp.float32),
            pltpu.VMEM((blocks // 2, rows, LANES), jnp.float32),
            pltpu.VMEM((blocks // 2, rows, LANES), jnp.float32),
            pltpu.VMEM((2, tall, LANES), jnp.float32),
            pltpu.VMEM((2, tall, LANES), jnp.float32),
            pltpu.SemaphoreType.DMA((9,)),
            pltpu.SemaphoreType.DMA((9,)),
        ],
        compiler_params=pltpu.CompilerParams(
            collective_id=1, has_side_effects=True, vmem_limit_bytes=52 * 1024 * 1024
        ),
    )(parent, nests, lateral, vertical)


def zone_kernel(counts, we_ref, sn_ref, we_out, sn_out, we_sum, sn_sum, we_in, sn_in,
                pair_send, pair_recv, we_send, we_recv, sn_send, sn_recv):
    tiles, groups, levs = counts
    chips = tiles * groups
    tile_at = lax.axis_index("tile")
    nest_at = lax.axis_index("nest")
    lev_at = lax.axis_index("lev")
    me = tile_at * groups + nest_at
    edge = (tile_at == 0) | (tile_at == tiles - 1)
    sibling = {"lev": 1 - lev_at}

    def chip(k):
        other = lax.rem(me + k, chips)
        return other, other // groups, lax.rem(other, groups)

    def we_copy(k):
        other, t, g = chip(k)
        return pltpu.make_async_remote_copy(
            src_ref=we_sum.at[other],
            dst_ref=we_in.at[k],
            send_sem=we_send.at[k],
            recv_sem=we_recv.at[k],
            device_id={"tile": t, "nest": g},
            device_id_type=MESH,
        )

    def sn_copy(k):
        other, t, g = chip(k)
        side = jnp.where(t == 0, 0, 1)
        return pltpu.make_async_remote_copy(
            src_ref=sn_sum.at[side * groups + g],
            dst_ref=sn_in.at[k],
            send_sem=sn_send.at[k],
            recv_sem=sn_recv.at[k],
            device_id={"tile": t, "nest": g},
            device_id_type=MESH,
        )

    def to_edge(k):
        other, t, g = chip(k)
        return (t == 0) | (t == tiles - 1)

    barrier = pltpu.get_barrier_semaphore()
    pl.semaphore_signal(barrier, inc=1, device_id=sibling, device_id_type=MESH)

    def greet(k, carry):
        other, t, g = chip(k)
        pl.semaphore_signal(
            barrier, inc=1, device_id={"tile": t, "nest": g}, device_id_type=MESH
        )
        return carry

    lax.fori_loop(1, chips, greet, 0)
    pl.semaphore_wait(barrier, chips)

    pairs = []
    for at, (src, dst) in enumerate(((sn_ref, sn_sum), (we_ref, we_sum))):
        pair = pltpu.make_async_remote_copy(
            src_ref=src.at[1 - lev_at],
            dst_ref=dst,
            send_sem=pair_send.at[at],
            recv_sem=pair_recv.at[at],
            device_id=sibling,
            device_id_type=MESH,
        )
        pair.start()
        pairs.append(pair)
    pairs[0].wait()
    sn_sum[...] += sn_ref[lev_at]

    def begin_sn(k, carry):
        pl.when(to_edge(k))(lambda: sn_copy(k).start())
        return carry

    lax.fori_loop(1, chips, begin_sn, 0)
    pairs[1].wait()
    we_sum[...] += we_ref[lev_at]

    def begin_we(k, carry):
        we_copy(k).start()
        return carry

    lax.fori_loop(1, chips, begin_we, 0)

    we_out[...] = we_sum[me]
    side_at = jnp.where(tile_at == 0, 0, 1)
    sn_out[...] = sn_sum[side_at * groups + nest_at]

    def finish(k, carry):
        pl.when(to_edge(k))(lambda: sn_copy(k).wait_send())

        @pl.when(edge)
        def _():
            sn_copy(k).wait_recv()
            sn_out[...] += sn_in[k]

        we_copy(k).wait()
        we_out[...] += we_in[k]
        return carry

    lax.fori_loop(1, chips, finish, 0)


def sum_zones(we, sn, counts):
    tiles, groups, levs = counts
    chips = tiles * groups
    room = 8 * 1024 * 1024 + 4 * sum(a.size * (2 * levs + 2) for a in (we, sn)) // levs
    vmem = pl.BlockSpec(memory_space=pltpu.VMEM)
    return pl.pallas_call(
        functools.partial(zone_kernel, counts),
        out_shape=(
            jax.ShapeDtypeStruct(we.shape[2:], jnp.float32),
            jax.ShapeDtypeStruct(sn.shape[2:], jnp.float32),
        ),
        in_specs=[vmem, vmem],
        out_specs=(vmem, vmem),
        scratch_shapes=[
            pltpu.VMEM(we.shape[1:], jnp.float32),
            pltpu.VMEM(sn.shape[1:], jnp.float32),
            pltpu.VMEM((chips,) + we.shape[2:], jnp.float32),
            pltpu.VMEM((chips,) + sn.shape[2:], jnp.float32),
            pltpu.SemaphoreType.DMA((2,)),
            pltpu.SemaphoreType.DMA((2,)),
            pltpu.SemaphoreType.DMA((chips,)),
            pltpu.SemaphoreType.DMA((chips,)),
            pltpu.SemaphoreType.DMA((chips,)),
            pltpu.SemaphoreType.DMA((chips,)),
        ],
        compiler_params=pltpu.CompilerParams(
            collective_id=0, has_side_effects=True, vmem_limit_bytes=room
        ),
    )(we, sn)


def nest_kernel(shape, steps, centres, storms, lateral, vertical, x_hbm, sn_ref, we_ref, o_hbm,
                x_ref, relaxed, state, done, col_mix, row_mix, load, sem):
    slots, fields, levels, rows, cols = shape
    planes = fields * levels
    high = x_ref.shape[2]
    edge = 8
    mid = high - 2 * edge

    def fetch(n):
        part = pl.ds(n * planes, planes)
        return pltpu.make_async_copy(x_hbm.at[part], x_ref.at[part], load.at[n])

    for n in range(slots):
        fetch(n).start()
    tile_at = lax.axis_index("tile")
    nest_at = lax.axis_index("nest")
    lev_at = lax.axis_index("lev")
    half = cols - LANES
    lane = lax.broadcasted_iota(jnp.int32, (mid, LANES), 1)
    row = lax.broadcasted_iota(jnp.int32, (mid, LANES), 0) + (tile_at * rows - HALO + edge)
    near = jnp.where(
        lev_at == 0, lane, jnp.where(lane < half, cols + LANES + lane, cols - LANES + lane)
    )
    far = jnp.where(lev_at == 0, LANES, cols) + lane
    col_lane = jnp.where(lev_at == 0, 0, half - 1)
    blocks = (HALO - edge, HALO - edge + rows - edge)

    def mixing(r, c, down, right):
        gap = jnp.minimum(jnp.minimum(r, SPAN - 1 - r), jnp.minimum(c, SPAN - 1 - c))
        weight = jnp.maximum(BORDER - gap, 0).astype(jnp.float32) / jnp.float32(BORDER)
        keep = (r + down >= 0) & (r + down < SPAN) & (c + right >= 0) & (c + right < SPAN)
        return jnp.where(keep, weight, 1.0)

    def patched(whole, blend):
        parts = []
        past = 0
        for at, start in enumerate(blocks):
            parts += [whole[past:start], blend(at, start, whole[start : start + edge])]
            past = start + edge
        return jnp.concatenate([a for a in parts + [whole[past:]] if a.shape[0]], axis=0)

    def one_nest(n, carry):
        shifts = []
        storm = storms[nest_at * slots + n]
        for step in range(steps):
            down = 3 * (centres[step + 1, storm, 0] - centres[step, storm, 0])
            right = 3 * (centres[step + 1, storm, 1] - centres[step, storm, 1])
            shifts.append((down, right))
            weight = mixing(row, near, down, right)
            side_row = (row < BORDER) | (row >= SPAN - BORDER)
            gap_c = jnp.minimum(near, SPAN - 1 - near)
            weight = jnp.where(side_row | (gap_c >= BORDER), 0.0, weight)
            second = ((near >= 3) & (near < BORDER)) | (near >= SPAN - 3)
            col_mix[step, 0] = 1.0 - weight
            col_mix[step, 1] = jnp.where(second, 0.0, weight)
            col_mix[step, 2] = jnp.where(second, weight, 0.0)
            for side in range(2):
                for at, start in enumerate(blocks):
                    r = row[start : start + edge]
                    c = (near, far)[side][start : start + edge]
                    weight = mixing(r, c, down, right)
                    weight = jnp.where((r < BORDER) | (r >= SPAN - BORDER), weight, 0.0)
                    second = ((r >= 3) & (r < BORDER)) | (r >= SPAN - 3)
                    row_mix[step, side, at, 0] = 1.0 - weight
                    row_mix[step, side, at, 1] = jnp.where(second, 0.0, weight)
                    row_mix[step, side, at, 2] = jnp.where(second, weight, 0.0)

        fetch(n).wait()

        def relax(step, f, v):
            down, right = shifts[step]
            k = 2 * step
            turn = lax.rem(LANES - right, LANES)
            own = (lane + right >= 0) & (lane + right < LANES)
            b = n * planes + f * levels + v
            spot = pl.ds(edge + down, mid)
            if step == 0:
                turned = [pltpu.roll(x_ref[b, side, spot, :], turn, 1) for side in range(2)]
            else:
                turned = [
                    pltpu.roll(state[f * levels + v, side, spot, :], turn, 1) for side in range(2)
                ]
            first = jnp.where(own, turned[0], turned[1])
            first = (
                col_mix[step, 0] * first
                + col_mix[step, 1] * we_ref[b, edge : edge + mid, k : k + 1]
                + col_mix[step, 2] * we_ref[b, edge : edge + mid, k + 1 : k + 2]
            )
            halves = (first, jnp.where(own, turned[1], turned[0]))
            for side in range(2):
                wide = slice(side * LANES, (side + 1) * LANES)

                def blend(at, start, block):
                    return (
                        row_mix[step, side, at, 0] * block
                        + row_mix[step, side, at, 1] * sn_ref[b, k : k + 1, wide]
                        + row_mix[step, side, at, 2] * sn_ref[b, k + 1 : k + 2, wide]
                    )

                relaxed[f * levels + v, side, edge : edge + mid] = patched(halves[side], blend)

        def diffuse(f, v):
            rate_l = lateral[f]
            rate_v = vertical[f]
            keep_rate = 1.0 - 4.0 * rate_l - 2.0 * rate_v
            p = f * levels + v
            here = [relaxed[p, side, edge : edge + mid] for side in range(2)]
            west = [pltpu.roll(a, 1, 1) for a in here]
            east = [pltpu.roll(a, LANES - 1, 1) for a in here]
            for side in range(2):
                around = (
                    relaxed[p, side, edge - 1 : edge - 1 + mid]
                    + relaxed[p, side, edge + 1 : edge + 1 + mid]
                    + jnp.where(lane == 0, west[1 - side], west[side])
                    + jnp.where(lane == LANES - 1, east[1 - side], east[side])
                )
                new = (
                    keep_rate * here[side]
                    + rate_l * around
                    + rate_v * relaxed[f * levels + 1 - v, side, edge : edge + mid]
                )
                if side == 0:
                    new = jnp.where(lane == col_lane, here[0], new)

                def blend(at, start, block):
                    r = row[start : start + edge]
                    before = here[side][start : start + edge]
                    return jnp.where((r == 0) | (r == SPAN - 1), before, block)

                state[p, side, edge : edge + mid] = patched(new, blend)

        for step in range(steps):
            for f in range(fields):
                for v in range(levels):
                    relax(step, f, v)
            for f in range(fields):
                for v in range(levels):
                    diffuse(f, v)
        for f in range(fields):
            for v in range(levels):
                near_part = state[f * levels + v, 0, HALO : HALO + rows]
                far_part = state[f * levels + v, 1, HALO : HALO + rows]
                done[n, f, v, :, :LANES] = jnp.where(lev_at == 0, near_part, far_part)
                done[n, f, v, :, LANES:] = jnp.where(lev_at == 0, far_part, near_part)[:, :half]
        pltpu.make_async_copy(done.at[n], o_hbm.at[n], sem.at[n]).start()
        return carry

    lax.fori_loop(0, slots, one_nest, 0)
    for n in range(slots):
        pltpu.make_async_copy(done.at[n], o_hbm.at[n], sem.at[n]).wait()


def advance_nests(wide_nests, along, across, centres, storms, lateral, vertical, shape, steps):
    slots, fields, levels, rows, cols = shape
    high = wide_nests.shape[2]
    vmem = pl.BlockSpec(memory_space=pltpu.VMEM)
    smem = pl.BlockSpec(memory_space=pltpu.SMEM)
    return pl.pallas_call(
        functools.partial(nest_kernel, shape, steps),
        out_shape=jax.ShapeDtypeStruct(shape, jnp.float32),
        in_specs=[smem] * 4 + [pl.BlockSpec(memory_space=pl.ANY)] + [vmem] * 2,
        out_specs=pl.BlockSpec(memory_space=pl.ANY),
        scratch_shapes=[
            pltpu.VMEM(wide_nests.shape, jnp.float32),
            pltpu.VMEM((fields * levels, 2, high, LANES), jnp.float32),
            pltpu.VMEM((fields * levels, 2, high, LANES), jnp.float32),
            pltpu.VMEM(shape, jnp.float32),
            pltpu.VMEM((steps, 3, high - 16, LANES), jnp.float32),
            pltpu.VMEM((steps, 2, 2, 3, 8, LANES), jnp.float32),
            pltpu.SemaphoreType.DMA((slots,)),
            pltpu.SemaphoreType.DMA((slots,)),
        ],
        compiler_params=pltpu.CompilerParams(vmem_limit_bytes=52 * 1024 * 1024),
    )(centres, storms, lateral, vertical, wide_nests, along, across)


def per_device(parent_field, nest_fields, lateral_rate, vertical_rate, centres, slot_storm):
    fields, levels, prow, pcol = parent_field.shape
    slots, _, _, rows, cols = nest_fields.shape
    storms = slot_storm.shape[0]
    steps = centres.shape[0] - 1
    tiles = lax.axis_size("tile")
    groups = lax.axis_size("nest")
    levs = lax.axis_size("lev")
    tile_at = lax.axis_index("tile")
    nest_at = lax.axis_index("nest")
    lev_at = lax.axis_index("lev")
    coarse = rows // 3
    assert levs == 2 and tiles > 1 and steps == 2 and levels == 2

    counts = (tiles, groups, levs)
    planes = fields * levels
    stages, wide_nests = exchange_halos(
        parent_field.reshape(planes, prow, pcol),
        nest_fields.reshape(slots * planes, rows, cols),
        lateral_rate,
        vertical_rate,
        counts,
    )
    high = wide_nests.shape[2]
    wide = 2 * LANES
    xg = tile_at * prow + jnp.arange(prow, dtype=jnp.int32)
    yg = (nest_at * levs + lev_at) * pcol + jnp.arange(pcol, dtype=jnp.int32)

    storm_ids = jnp.arange(storms, dtype=jnp.int32)
    pick = (slot_storm[:, None] == storm_ids[None, :]).astype(jnp.int32)
    place_at = jnp.sum(pick[None, :, :, None] * centres[:, None, :, :], axis=2)

    edges = jnp.array([0, 1, FP - 2, FP - 1], jnp.int32)
    deep = coarse + 8
    rows_at = (jnp.arange(tiles, dtype=jnp.int32) * coarse - 4)[:, None] + jnp.arange(deep, dtype=jnp.int32)
    rows_at = jnp.where((rows_at >= 0) & (rows_at < FP), rows_at, -SPAN * SPAN)
    lanes = -(-slots * ALONG // LANES) * LANES
    lane = jnp.arange(lanes, dtype=jnp.int32)
    starts = jnp.array([0, FP - ALONG], jnp.int32)
    along_at = starts[None, :, None] + lane - ALONG * jnp.arange(slots, dtype=jnp.int32)[:, None, None]
    own_lane = lane // ALONG == jnp.arange(slots, dtype=jnp.int32)[:, None, None]
    along_at = jnp.where(own_lane, along_at, -SPAN * SPAN)
    corner = place_at[1:] - FP // 2
    corner_r, corner_c = corner[:, :, 0, None, None], corner[:, :, 1, None, None]
    row_edge = (corner_r + edges[:, None] == xg).astype(jnp.float32)
    col_edge = (corner_c + edges[:, None] == yg).astype(jnp.float32)
    col_at = corner[:, :, 1].reshape(steps, groups, slots, 1, 1, 1) + along_at[:, :, None, :]
    col_pick = (col_at == yg[:, None]).astype(jnp.float32)
    row_pick = (corner_r[..., None] + rows_at[:, :, None] == xg).astype(jnp.float32)
    sn = jnp.einsum("sjrx,sfxy->sjrfy", row_edge, stages, precision=EXACT)
    sn = sn.reshape(steps, groups, slots, 2, 2, planes, pcol)
    sn = jnp.einsum("sgnhkfy,sgnlyc->lhgskfc", sn, col_pick, precision=EXACT)
    sn = sn.reshape(levs, 2 * groups, steps * 2 * planes, lanes)
    we = jnp.einsum("sjky,sfxy->sjkfx", col_edge, stages, precision=EXACT)
    we = jnp.einsum("sjtrx,sjkfx->sjtrkf", row_pick, we, precision=EXACT)
    we = we.reshape(steps, groups, slots, tiles, deep, levs, 2, planes)
    we = jnp.transpose(we, (5, 3, 1, 4, 2, 6, 0, 7))
    we = we.reshape(levs, tiles * groups, deep, slots * 2 * steps * planes)
    we = jnp.pad(we, ((0, 0), (0, 0), (0, 0), (0, -we.shape[3] % LANES)))
    we, sn = sum_zones(we, sn, counts)

    jj = jnp.arange(wide, dtype=jnp.int32)
    swapped = jnp.where(jj < cols - LANES, cols + LANES + jj, cols - LANES + jj)
    swapped = jnp.where(jj < LANES, swapped, cols - LANES + jj)
    col_cell = jnp.where(lev_at == 0, jj, swapped)
    row_cell = tile_at * rows - HALO + jnp.arange(high, dtype=jnp.int32)
    from_col = col_cell // 3 - lev_at * (FP - ALONG)
    spread_c = (own_lane[:, 0, :, None] & (from_col == (lane % ALONG)[:, None])).astype(jnp.float32)
    from_row = row_cell // 3 - (tile_at * coarse - 4)
    spread_r = (from_row[:, None] == jnp.arange(deep, dtype=jnp.int32)).astype(jnp.float32)
    along = jnp.einsum("ql,nlc->nqc", sn, spread_c, precision=EXACT)
    along = along.reshape(slots, 2 * steps, fields, levels, wide)
    along = jnp.transpose(along, (0, 2, 3, 1, 4)).reshape(slots * planes, 2 * steps, wide)
    across = jnp.einsum("rq,qm->rm", spread_r, we, precision=EXACT)
    across = across[:, : slots * 2 * steps * planes].reshape(high, slots, 2, steps, fields, levels)
    across = jnp.transpose(across, (1, 4, 5, 0, 3, 2)).reshape(slots * planes, high, 2 * steps)
    nests = advance_nests(
        wide_nests,
        along,
        across,
        centres,
        slot_storm,
        lateral_rate,
        vertical_rate,
        nest_fields.shape,
        steps,
    )
    return (stages[1].reshape(parent_field.shape), nests)


def solution(mesh):
    placed = (
        P("member", None, "tile", ("nest", "lev")),
        P(("member", "nest"), None, None, "tile", "lev"),
        P(),
        P(),
        P("member", None, None),
        P("member"),
    )
    return jax.shard_map(
        per_device,
        mesh=mesh,
        in_specs=placed,
        out_specs=(
            P("member", None, "tile", ("nest", "lev")),
            P(("member", "nest"), None, None, "tile", "lev"),
        ),
        check_vma=False,
    )
```

```python
import functools
import jax
import jax.numpy as jnp
from jax import lax
from jax.experimental import pallas as pl
from jax.experimental.pallas import tpu as pltpu
from jax.sharding import PartitionSpec as P

FP = 128
BWP = 2
MOVE = 2
HALO = 16
LANES = 128
ALONG = 72
SPAN = 3 * FP
BORDER = 3 * BWP
EXACT = lax.Precision.HIGHEST


MESH = pl.DeviceIdType.MESH


def halo_kernel(counts, p_hbm, n_hbm, rates, stage_ref, w_hbm,
                p_ref, n_ref, w_ref, load, field, side, pack, held, cols_out, cols_in, send, recv):
    tiles, groups, levs = counts
    tile_at = lax.axis_index("tile")
    nest_at = lax.axis_index("nest")
    lev_at = lax.axis_index("lev")
    planes, prow, pcol = p_ref.shape
    blocks, rows, cols = n_ref.shape
    half = cols - LANES
    edge = 8
    above = tile_at > 0
    below = tile_at < tiles - 1
    beyond = ((lev_at == 0) & (nest_at > 0)) | ((lev_at == 1) & (nest_at < groups - 1))
    step_out = 2 * lev_at - 1
    sibling = {"lev": 1 - lev_at}
    outer = {"nest": jnp.clip(nest_at + step_out, 0, groups - 1), "lev": 1 - lev_at}
    upper = {"tile": jnp.maximum(tile_at - 1, 0)}
    lower = {"tile": jnp.minimum(tile_at + 1, tiles - 1)}

    def remote(src, dst, at, landing, place):
        return pltpu.make_async_remote_copy(
            src_ref=src,
            dst_ref=dst,
            send_sem=send.at[at],
            recv_sem=recv.at[landing],
            device_id=place,
            device_id_type=MESH,
        )

    load_parent = pltpu.make_async_copy(p_hbm, p_ref, load.at[0])
    load_nests = pltpu.make_async_copy(n_hbm, n_ref, load.at[1])
    load_parent.start()
    load_nests.start()
    barrier = pltpu.get_barrier_semaphore()

    def greet(place):
        pl.semaphore_signal(barrier, inc=1, device_id=place, device_id_type=MESH)

    greet(sibling)
    pl.when(above)(lambda: greet(upper))
    pl.when(below)(lambda: greet(lower))
    pl.when(beyond)(lambda: greet(outer))
    pl.semaphore_wait(
        barrier,
        1 + above.astype(jnp.int32) + below.astype(jnp.int32) + beyond.astype(jnp.int32),
    )

    load_parent.wait()
    rows_up = remote(p_ref.at[:, pl.ds(0, edge)], field.at[:, pl.ds(prow + edge, edge)], 0, 0, upper)
    rows_down = remote(p_ref.at[:, pl.ds(prow - edge, edge)], field.at[:, pl.ds(0, edge)], 1, 1, lower)
    pl.when(above)(rows_up.start)
    pl.when(below)(rows_down.start)

    load_nests.wait()
    own_up = remote(
        n_ref.at[:, pl.ds(0, HALO), pl.ds(0, LANES)],
        w_ref.at[:, lev_at, pl.ds(HALO + rows, HALO)],
        7, 7, upper,
    )
    own_down = remote(
        n_ref.at[:, pl.ds(rows - HALO, HALO), pl.ds(0, LANES)],
        w_ref.at[:, lev_at, pl.ds(0, HALO)],
        8, 8, lower,
    )
    pl.when(above)(own_up.start)
    pl.when(below)(own_down.start)

    def gather(i, carry):
        def nearer(b):
            return jnp.where(lev_at == 0, n_ref[b, :, LANES:], n_ref[b, :, :half])

        pack[i] = jnp.concatenate([nearer(2 * i), nearer(2 * i + 1)], axis=1)
        return carry

    lax.fori_loop(0, blocks // 2, gather, 0)
    across = remote(pack, held, 4, 4, sibling)
    across.start()

    field[:, edge : edge + prow, :] = p_ref[...]

    @pl.when(jnp.logical_not(above))
    def _():
        field[:, :edge, :] = jnp.zeros((planes, edge, pcol), jnp.float32)

    @pl.when(jnp.logical_not(below))
    def _():
        field[:, prow + edge :, :] = jnp.zeros((planes, edge, pcol), jnp.float32)

    pl.when(above)(rows_up.wait_send)
    pl.when(below)(rows_down.wait_send)
    pl.when(below)(rows_up.wait_recv)
    pl.when(above)(rows_down.wait_recv)

    tall = prow + 2 * edge
    lane = lax.broadcasted_iota(jnp.int32, (tall, LANES), 1)
    first = jnp.zeros((tall, LANES), jnp.float32)
    last = jnp.zeros((tall, LANES), jnp.float32)
    for f in range(planes):
        mine = (lane == 2 * f) | (lane == 2 * f + 1)
        here = field[f]
        first = jnp.where(mine, pltpu.roll(here, 2 * f, 1) if f else here, first)
        last = jnp.where(mine, pltpu.roll(here, 2 * f + 2, 1), last)
    cols_out[0] = jnp.where(lev_at == 0, last, first)
    cols_out[1] = jnp.where(lev_at == 0, first, last)
    to_sibling = remote(cols_out.at[0], cols_in.at[0], 2, 2, sibling)
    to_outer = remote(cols_out.at[1], cols_in.at[1], 3, 3, outer)
    to_sibling.start()
    pl.when(beyond)(to_outer.start)

    @pl.when(jnp.logical_not(beyond))
    def _():
        cols_in[1] = jnp.zeros((tall, LANES), jnp.float32)

    across.wait()

    def widen(i, carry):
        both = held[i]
        for o in range(2):
            b = 2 * i + o
            whole = n_ref[b, :, :LANES]
            mixed = jnp.concatenate([n_ref[b, :, LANES:], both[:, o * half : (o + 1) * half]], axis=1)
            w_ref[b, 0, HALO : HALO + rows, :] = jnp.where(lev_at == 0, whole, mixed)
            w_ref[b, 1, HALO : HALO + rows, :] = jnp.where(lev_at == 0, mixed, whole)
        return carry

    lax.fori_loop(0, blocks // 2, widen, 0)
    mixed_at = 1 - lev_at
    nest_up = remote(
        w_ref.at[:, mixed_at, pl.ds(HALO, HALO)],
        w_ref.at[:, mixed_at, pl.ds(HALO + rows, HALO)],
        5, 5, upper,
    )
    nest_down = remote(
        w_ref.at[:, mixed_at, pl.ds(rows, HALO)], w_ref.at[:, mixed_at, pl.ds(0, HALO)], 6, 6, lower
    )
    pl.when(above)(nest_up.start)
    pl.when(below)(nest_down.start)

    @pl.when(jnp.logical_not(above))
    def _():
        w_ref[:, :, :HALO, :] = jnp.zeros((blocks, 2, HALO, LANES), jnp.float32)

    @pl.when(jnp.logical_not(below))
    def _():
        w_ref[:, :, HALO + rows :, :] = jnp.zeros((blocks, 2, HALO, LANES), jnp.float32)

    to_sibling.wait()
    pl.when(beyond)(to_outer.wait)
    left = jnp.where(lev_at == 0, cols_in[1], cols_in[0])
    right = jnp.where(lev_at == 0, cols_in[0], cols_in[1])
    for f in range(planes):
        after = pltpu.roll(right, LANES - 2 * f, 1) if f else right
        before = pltpu.roll(left, LANES - 2 - 2 * f, 1)
        side[f] = jnp.where(lane < 2, after, jnp.where(lane >= LANES - 2, before, 0.0))

    wide = 2 * LANES
    x = tile_at * prow - edge + lax.broadcasted_iota(jnp.int32, (tall, wide), 0)
    y = lax.broadcasted_iota(jnp.int32, (tall, wide), 1)
    y = (nest_at * levs + lev_at) * pcol + jnp.where(y >= LANES + 2, y - wide, y)
    domain = (x >= 0) & (x < prow * tiles) & (y >= 0) & (y < pcol * groups * levs)

    def advance(i, carry):
        rate_l = rates[0, i]
        rate_v = rates[1, i]
        now = [jnp.concatenate([field[2 * i + v], side[2 * i + v]], axis=1) for v in range(2)]
        for step in range(2):
            later = []
            for v in range(2):
                here = now[v]
                around = (
                    pltpu.roll(here, 1, 0)
                    + pltpu.roll(here, tall - 1, 0)
                    + pltpu.roll(here, 1, 1)
                    + pltpu.roll(here, wide - 1, 1)
                    - 4.0 * here
                )
                change = rate_l * around + rate_v * (now[1 - v] - 2.0 * here)
                later.append(jnp.where(domain, here + change, 0.0))
            now = later
            for v in range(2):
                stage_ref[step, 2 * i + v] = now[v][edge : edge + prow, :pcol]
        return carry

    lax.fori_loop(0, planes // 2, advance, 0)

    def keep(at, start, size):
        return pltpu.make_async_copy(
            w_ref.at[:, :, pl.ds(start, size)], w_hbm.at[:, :, pl.ds(start, size)], load.at[at]
        )

    middle = keep(0, HALO, rows)
    middle.start()
    for up, down in ((own_up, own_down), (nest_up, nest_down)):
        pl.when(above)(up.wait_send)
        pl.when(below)(down.wait_send)
        pl.when(below)(up.wait_recv)
        pl.when(above)(down.wait_recv)
    head = keep(1, 0, HALO)
    tail = keep(2, HALO + rows, HALO)
    head.start()
    tail.start()
    middle.wait()
    head.wait()
    tail.wait()


def exchange_halos(parent, nests, rates, counts):
    planes, prow, pcol = parent.shape
    blocks, rows, cols = nests.shape
    assert pcol == LANES and planes % 2 == 0 and blocks % 2 == 0 and 2 * (cols - LANES) == LANES
    vmem = pl.BlockSpec(memory_space=pltpu.VMEM)
    smem = pl.BlockSpec(memory_space=pltpu.SMEM)
    anywhere = pl.BlockSpec(memory_space=pl.ANY)
    tall = prow + 16
    shape = lambda *dims: jax.ShapeDtypeStruct(dims, jnp.float32)
    return pl.pallas_call(
        functools.partial(halo_kernel, counts),
        out_shape=(
            shape(2, planes, prow, pcol),
            shape(blocks, 2, rows + 2 * HALO, LANES),
        ),
        in_specs=[anywhere, anywhere, smem],
        out_specs=(vmem, anywhere),
        scratch_shapes=[
            pltpu.VMEM((planes, prow, pcol), jnp.float32),
            pltpu.VMEM((blocks, rows, cols), jnp.float32),
            pltpu.VMEM((blocks, 2, rows + 2 * HALO, LANES), jnp.float32),
            pltpu.SemaphoreType.DMA((3,)),
            pltpu.VMEM((planes, tall, LANES), jnp.float32),
            pltpu.VMEM((planes, tall, LANES), jnp.float32),
            pltpu.VMEM((blocks // 2, rows, LANES), jnp.float32),
            pltpu.VMEM((blocks // 2, rows, LANES), jnp.float32),
            pltpu.VMEM((2, tall, LANES), jnp.float32),
            pltpu.VMEM((2, tall, LANES), jnp.float32),
            pltpu.SemaphoreType.DMA((9,)),
            pltpu.SemaphoreType.DMA((9,)),
        ],
        compiler_params=pltpu.CompilerParams(
            collective_id=1, has_side_effects=True, vmem_limit_bytes=52 * 1024 * 1024
        ),
    )(parent, nests, rates)


def zone_kernel(counts, we_ref, sn_ref, we_out, sn_out, we_sum, sn_sum, we_in, sn_in,
                pair_send, pair_recv, we_send, we_recv, sn_send, sn_recv):
    tiles, groups, levs = counts
    chips = tiles * groups
    tile_at = lax.axis_index("tile")
    nest_at = lax.axis_index("nest")
    lev_at = lax.axis_index("lev")
    me = tile_at * groups + nest_at
    edge = (tile_at == 0) | (tile_at == tiles - 1)
    sibling = {"lev": 1 - lev_at}

    def chip(k):
        other = lax.rem(me + k, chips)
        return other, other // groups, lax.rem(other, groups)

    def we_copy(k):
        other, t, g = chip(k)
        return pltpu.make_async_remote_copy(
            src_ref=we_sum.at[other],
            dst_ref=we_in.at[k],
            send_sem=we_send.at[k],
            recv_sem=we_recv.at[k],
            device_id={"tile": t, "nest": g},
            device_id_type=MESH,
        )

    def sn_copy(k):
        other, t, g = chip(k)
        side = jnp.where(t == 0, 0, 1)
        return pltpu.make_async_remote_copy(
            src_ref=sn_sum.at[side * groups + g],
            dst_ref=sn_in.at[k],
            send_sem=sn_send.at[k],
            recv_sem=sn_recv.at[k],
            device_id={"tile": t, "nest": g},
            device_id_type=MESH,
        )

    def to_edge(k):
        other, t, g = chip(k)
        return (t == 0) | (t == tiles - 1)

    barrier = pltpu.get_barrier_semaphore()
    pl.semaphore_signal(barrier, inc=1, device_id=sibling, device_id_type=MESH)

    def greet(k, carry):
        other, t, g = chip(k)
        pl.semaphore_signal(
            barrier, inc=1, device_id={"tile": t, "nest": g}, device_id_type=MESH
        )
        return carry

    lax.fori_loop(1, chips, greet, 0)
    pl.semaphore_wait(barrier, chips)

    pairs = []
    for at, (src, dst) in enumerate(((sn_ref, sn_sum), (we_ref, we_sum))):
        pair = pltpu.make_async_remote_copy(
            src_ref=src.at[1 - lev_at],
            dst_ref=dst,
            send_sem=pair_send.at[at],
            recv_sem=pair_recv.at[at],
            device_id=sibling,
            device_id_type=MESH,
        )
        pair.start()
        pairs.append(pair)
    pairs[0].wait()
    sn_sum[...] += sn_ref[lev_at]

    def begin_sn(k, carry):
        pl.when(to_edge(k))(lambda: sn_copy(k).start())
        return carry

    lax.fori_loop(1, chips, begin_sn, 0)
    pairs[1].wait()
    we_sum[...] += we_ref[lev_at]

    def begin_we(k, carry):
        we_copy(k).start()
        return carry

    lax.fori_loop(1, chips, begin_we, 0)

    we_out[...] = we_sum[me]
    side_at = jnp.where(tile_at == 0, 0, 1)
    sn_out[...] = sn_sum[side_at * groups + nest_at]

    def finish(k, carry):
        pl.when(to_edge(k))(lambda: sn_copy(k).wait_send())

        @pl.when(edge)
        def _():
            sn_copy(k).wait_recv()
            sn_out[...] += sn_in[k]

        we_copy(k).wait()
        we_out[...] += we_in[k]
        return carry

    lax.fori_loop(1, chips, finish, 0)


def sum_zones(we, sn, counts):
    tiles, groups, levs = counts
    chips = tiles * groups
    room = 8 * 1024 * 1024 + 4 * sum(a.size * (2 * levs + 2) for a in (we, sn)) // levs
    vmem = pl.BlockSpec(memory_space=pltpu.VMEM)
    return pl.pallas_call(
        functools.partial(zone_kernel, counts),
        out_shape=(
            jax.ShapeDtypeStruct(we.shape[2:], jnp.float32),
            jax.ShapeDtypeStruct(sn.shape[2:], jnp.float32),
        ),
        in_specs=[vmem, vmem],
        out_specs=(vmem, vmem),
        scratch_shapes=[
            pltpu.VMEM(we.shape[1:], jnp.float32),
            pltpu.VMEM(sn.shape[1:], jnp.float32),
            pltpu.VMEM((chips,) + we.shape[2:], jnp.float32),
            pltpu.VMEM((chips,) + sn.shape[2:], jnp.float32),
            pltpu.SemaphoreType.DMA((2,)),
            pltpu.SemaphoreType.DMA((2,)),
            pltpu.SemaphoreType.DMA((chips,)),
            pltpu.SemaphoreType.DMA((chips,)),
            pltpu.SemaphoreType.DMA((chips,)),
            pltpu.SemaphoreType.DMA((chips,)),
        ],
        compiler_params=pltpu.CompilerParams(
            collective_id=0, has_side_effects=True, vmem_limit_bytes=room
        ),
    )(we, sn)


def nest_kernel(shape, steps, centres, storms, rates, x_hbm, sn_ref, we_ref, o_hbm,
                x_ref, relaxed, state, done, col_mix, row_mix, load, sem):
    slots, fields, levels, rows, cols = shape
    planes = fields * levels
    high = x_ref.shape[2]
    edge = 8
    mid = high - 2 * edge

    def fetch(n):
        part = pl.ds(n * planes, planes)
        return pltpu.make_async_copy(x_hbm.at[part], x_ref.at[part], load.at[n])

    for n in range(slots):
        fetch(n).start()
    tile_at = lax.axis_index("tile")
    nest_at = lax.axis_index("nest")
    lev_at = lax.axis_index("lev")
    half = cols - LANES
    lane = lax.broadcasted_iota(jnp.int32, (mid, LANES), 1)
    row = lax.broadcasted_iota(jnp.int32, (mid, LANES), 0) + (tile_at * rows - HALO + edge)
    near = jnp.where(
        lev_at == 0, lane, jnp.where(lane < half, cols + LANES + lane, cols - LANES + lane)
    )
    far = jnp.where(lev_at == 0, LANES, cols) + lane
    col_lane = jnp.where(lev_at == 0, 0, half - 1)
    blocks = (HALO - edge, HALO - edge + rows - edge)

    def mixing(r, c, down, right):
        gap = jnp.minimum(jnp.minimum(r, SPAN - 1 - r), jnp.minimum(c, SPAN - 1 - c))
        weight = jnp.maximum(BORDER - gap, 0).astype(jnp.float32) / jnp.float32(BORDER)
        keep = (r + down >= 0) & (r + down < SPAN) & (c + right >= 0) & (c + right < SPAN)
        return jnp.where(keep, weight, 1.0)

    def patched(whole, blend):
        parts = []
        past = 0
        for at, start in enumerate(blocks):
            parts += [whole[past:start], blend(at, start, whole[start : start + edge])]
            past = start + edge
        return jnp.concatenate([a for a in parts + [whole[past:]] if a.shape[0]], axis=0)

    def one_nest(n, carry):
        shifts = []
        storm = storms[nest_at * slots + n]
        for step in range(steps):
            down = 3 * (centres[step + 1, storm, 0] - centres[step, storm, 0])
            right = 3 * (centres[step + 1, storm, 1] - centres[step, storm, 1])
            shifts.append((down, right))
            weight = mixing(row, near, down, right)
            side_row = (row < BORDER) | (row >= SPAN - BORDER)
            gap_c = jnp.minimum(near, SPAN - 1 - near)
            weight = jnp.where(side_row | (gap_c >= BORDER), 0.0, weight)
            second = ((near >= 3) & (near < BORDER)) | (near >= SPAN - 3)
            col_mix[step, 0] = 1.0 - weight
            col_mix[step, 1] = jnp.where(second, 0.0, weight)
            col_mix[step, 2] = jnp.where(second, weight, 0.0)
            for side in range(2):
                for at, start in enumerate(blocks):
                    r = row[start : start + edge]
                    c = (near, far)[side][start : start + edge]
                    weight = mixing(r, c, down, right)
                    weight = jnp.where((r < BORDER) | (r >= SPAN - BORDER), weight, 0.0)
                    second = ((r >= 3) & (r < BORDER)) | (r >= SPAN - 3)
                    row_mix[step, side, at, 0] = 1.0 - weight
                    row_mix[step, side, at, 1] = jnp.where(second, 0.0, weight)
                    row_mix[step, side, at, 2] = jnp.where(second, weight, 0.0)

        fetch(n).wait()

        def relax(step, f, v):
            down, right = shifts[step]
            k = 2 * step
            turn = lax.rem(LANES - right, LANES)
            own = (lane + right >= 0) & (lane + right < LANES)
            b = n * planes + f * levels + v
            spot = pl.ds(edge + down, mid)
            if step == 0:
                turned = [pltpu.roll(x_ref[b, side, spot, :], turn, 1) for side in range(2)]
            else:
                turned = [
                    pltpu.roll(state[f * levels + v, side, spot, :], turn, 1) for side in range(2)
                ]
            first = jnp.where(own, turned[0], turned[1])
            first = (
                col_mix[step, 0] * first
                + col_mix[step, 1] * we_ref[b, edge : edge + mid, k : k + 1]
                + col_mix[step, 2] * we_ref[b, edge : edge + mid, k + 1 : k + 2]
            )
            halves = (first, jnp.where(own, turned[1], turned[0]))
            for side in range(2):
                wide = slice(side * LANES, (side + 1) * LANES)

                def blend(at, start, block):
                    return (
                        row_mix[step, side, at, 0] * block
                        + row_mix[step, side, at, 1] * sn_ref[b, k : k + 1, wide]
                        + row_mix[step, side, at, 2] * sn_ref[b, k + 1 : k + 2, wide]
                    )

                relaxed[f * levels + v, side, edge : edge + mid] = patched(halves[side], blend)

        def diffuse(f, v):
            rate_l = rates[0, f]
            rate_v = rates[1, f]
            keep_rate = 1.0 - 4.0 * rate_l - 2.0 * rate_v
            p = f * levels + v
            here = [relaxed[p, side, edge : edge + mid] for side in range(2)]
            west = [pltpu.roll(a, 1, 1) for a in here]
            east = [pltpu.roll(a, LANES - 1, 1) for a in here]
            for side in range(2):
                around = (
                    relaxed[p, side, edge - 1 : edge - 1 + mid]
                    + relaxed[p, side, edge + 1 : edge + 1 + mid]
                    + jnp.where(lane == 0, west[1 - side], west[side])
                    + jnp.where(lane == LANES - 1, east[1 - side], east[side])
                )
                new = (
                    keep_rate * here[side]
                    + rate_l * around
                    + rate_v * relaxed[f * levels + 1 - v, side, edge : edge + mid]
                )
                if side == 0:
                    new = jnp.where(lane == col_lane, here[0], new)

                def blend(at, start, block):
                    r = row[start : start + edge]
                    before = here[side][start : start + edge]
                    return jnp.where((r == 0) | (r == SPAN - 1), before, block)

                state[p, side, edge : edge + mid] = patched(new, blend)

        for step in range(steps):
            for f in range(fields):
                for v in range(levels):
                    relax(step, f, v)
            for f in range(fields):
                for v in range(levels):
                    diffuse(f, v)
        for f in range(fields):
            for v in range(levels):
                near_part = state[f * levels + v, 0, HALO : HALO + rows]
                far_part = state[f * levels + v, 1, HALO : HALO + rows]
                done[n, f, v, :, :LANES] = jnp.where(lev_at == 0, near_part, far_part)
                done[n, f, v, :, LANES:] = jnp.where(lev_at == 0, far_part, near_part)[:, :half]
        pltpu.make_async_copy(done.at[n], o_hbm.at[n], sem.at[n]).start()
        return carry

    lax.fori_loop(0, slots, one_nest, 0)
    for n in range(slots):
        pltpu.make_async_copy(done.at[n], o_hbm.at[n], sem.at[n]).wait()


def advance_nests(wide_nests, along, across, centres, storms, rates, shape, steps):
    slots, fields, levels, rows, cols = shape
    high = wide_nests.shape[2]
    vmem = pl.BlockSpec(memory_space=pltpu.VMEM)
    smem = pl.BlockSpec(memory_space=pltpu.SMEM)
    return pl.pallas_call(
        functools.partial(nest_kernel, shape, steps),
        out_shape=jax.ShapeDtypeStruct(shape, jnp.float32),
        in_specs=[smem] * 3 + [pl.BlockSpec(memory_space=pl.ANY)] + [vmem] * 2,
        out_specs=pl.BlockSpec(memory_space=pl.ANY),
        scratch_shapes=[
            pltpu.VMEM(wide_nests.shape, jnp.float32),
            pltpu.VMEM((fields * levels, 2, high, LANES), jnp.float32),
            pltpu.VMEM((fields * levels, 2, high, LANES), jnp.float32),
            pltpu.VMEM(shape, jnp.float32),
            pltpu.VMEM((steps, 3, high - 16, LANES), jnp.float32),
            pltpu.VMEM((steps, 2, 2, 3, 8, LANES), jnp.float32),
            pltpu.SemaphoreType.DMA((slots,)),
            pltpu.SemaphoreType.DMA((slots,)),
        ],
        compiler_params=pltpu.CompilerParams(vmem_limit_bytes=50 * 1024 * 1024),
    )(centres, storms, rates, wide_nests, along, across)


def per_device(parent_field, nest_fields, lateral_rate, vertical_rate, centres, slot_storm):
    fields, levels, prow, pcol = parent_field.shape
    slots, _, _, rows, cols = nest_fields.shape
    storms = slot_storm.shape[0]
    steps = centres.shape[0] - 1
    tiles = lax.axis_size("tile")
    groups = lax.axis_size("nest")
    levs = lax.axis_size("lev")
    tile_at = lax.axis_index("tile")
    nest_at = lax.axis_index("nest")
    lev_at = lax.axis_index("lev")
    coarse = rows // 3
    assert levs == 2 and tiles > 1 and steps == 2 and levels == 2

    counts = (tiles, groups, levs)
    planes = fields * levels
    rates = jnp.stack([lateral_rate, vertical_rate])
    stages, wide_nests = exchange_halos(
        parent_field.reshape(planes, prow, pcol),
        nest_fields.reshape(slots * planes, rows, cols),
        rates,
        counts,
    )
    high = wide_nests.shape[2]
    wide = 2 * LANES
    xg = tile_at * prow + jnp.arange(prow, dtype=jnp.int32)
    yg = (nest_at * levs + lev_at) * pcol + jnp.arange(pcol, dtype=jnp.int32)

    storm_ids = jnp.arange(storms, dtype=jnp.int32)
    pick = (slot_storm[:, None] == storm_ids[None, :]).astype(jnp.int32)
    place_at = jnp.sum(pick[None, :, :, None] * centres[:, None, :, :], axis=2)

    edges = jnp.array([0, 1, FP - 2, FP - 1], jnp.int32)
    deep = coarse + 8
    rows_at = (jnp.arange(tiles, dtype=jnp.int32) * coarse - 4)[:, None] + jnp.arange(deep, dtype=jnp.int32)
    rows_at = jnp.where((rows_at >= 0) & (rows_at < FP), rows_at, -SPAN * SPAN)
    lanes = -(-slots * ALONG // LANES) * LANES
    lane = jnp.arange(lanes, dtype=jnp.int32)
    starts = jnp.array([0, FP - ALONG], jnp.int32)
    along_at = starts[None, :, None] + lane - ALONG * jnp.arange(slots, dtype=jnp.int32)[:, None, None]
    own_lane = lane // ALONG == jnp.arange(slots, dtype=jnp.int32)[:, None, None]
    along_at = jnp.where(own_lane, along_at, -SPAN * SPAN)
    corner = place_at[1:] - FP // 2
    corner_r, corner_c = corner[:, :, 0, None, None], corner[:, :, 1, None, None]
    row_edge = (corner_r + edges[:, None] == xg).astype(jnp.float32)
    col_edge = (corner_c + edges[:, None] == yg).astype(jnp.float32)
    col_at = corner[:, :, 1].reshape(steps, groups, slots, 1, 1, 1) + along_at[:, :, None, :]
    col_pick = (col_at == yg[:, None]).astype(jnp.float32)
    row_pick = (corner_r[..., None] + rows_at[:, :, None] == xg).astype(jnp.float32)
    sn = jnp.einsum("sjrx,sfxy->sjrfy", row_edge, stages, precision=EXACT)
    sn = sn.reshape(steps, groups, slots, 2, 2, planes, pcol)
    sn = jnp.einsum("sgnhkfy,sgnlyc->lhgskfc", sn, col_pick, precision=EXACT)
    sn = sn.reshape(levs, 2 * groups, steps * 2 * planes, lanes)
    we = jnp.einsum("sjky,sfxy->sjkfx", col_edge, stages, precision=EXACT)
    we = jnp.einsum("sjtrx,sjkfx->sjtrkf", row_pick, we, precision=EXACT)
    we = we.reshape(steps, groups, slots, tiles, deep, levs, 2, planes)
    we = jnp.transpose(we, (5, 3, 1, 4, 2, 6, 0, 7))
    we = we.reshape(levs, tiles * groups, deep, slots * 2 * steps * planes)
    we = jnp.pad(we, ((0, 0), (0, 0), (0, 0), (0, -we.shape[3] % LANES)))
    we, sn = sum_zones(we, sn, counts)

    jj = jnp.arange(wide, dtype=jnp.int32)
    swapped = jnp.where(jj < cols - LANES, cols + LANES + jj, cols - LANES + jj)
    swapped = jnp.where(jj < LANES, swapped, cols - LANES + jj)
    col_cell = jnp.where(lev_at == 0, jj, swapped)
    row_cell = tile_at * rows - HALO + jnp.arange(high, dtype=jnp.int32)
    from_col = col_cell // 3 - lev_at * (FP - ALONG)
    spread_c = (own_lane[:, 0, :, None] & (from_col == (lane % ALONG)[:, None])).astype(jnp.float32)
    from_row = row_cell // 3 - (tile_at * coarse - 4)
    spread_r = (from_row[:, None] == jnp.arange(deep, dtype=jnp.int32)).astype(jnp.float32)
    along = jnp.einsum("ql,nlc->nqc", sn, spread_c, precision=EXACT)
    along = along.reshape(slots, 2 * steps, fields, levels, wide)
    along = jnp.transpose(along, (0, 2, 3, 1, 4)).reshape(slots * planes, 2 * steps, wide)
    across = jnp.einsum("rq,qm->rm", spread_r, we, precision=EXACT)
    across = across[:, : slots * 2 * steps * planes].reshape(high, slots, 2, steps, fields, levels)
    across = jnp.transpose(across, (1, 4, 5, 0, 3, 2)).reshape(slots * planes, high, 2 * steps)
    nests = advance_nests(
        wide_nests,
        along,
        across,
        centres,
        slot_storm,
        rates,
        nest_fields.shape,
        steps,
    )
    return (stages[1].reshape(parent_field.shape), nests)


def solution(mesh):
    placed = (
        P("member", None, "tile", ("nest", "lev")),
        P(("member", "nest"), None, None, "tile", "lev"),
        P(),
        P(),
        P("member", None, None),
        P("member"),
    )
    return jax.shard_map(
        per_device,
        mesh=mesh,
        in_specs=placed,
        out_specs=(
            P("member", None, "tile", ("nest", "lev")),
            P(("member", "nest"), None, None, "tile", "lev"),
        ),
        check_vma=False,
    )
```
